32 devices in a mesh: dp: 8 (over z, y), mp: 4 (over x, core).
Axes of the slice: x: 2, y: 2, z: 4, core: 2. Of those that a mesh axis runs over, the one named last changes fastest.
Arguments:
- queries: bfloat16 [1536, 4096], P('dp', 'mp'), as said below
- passages: bfloat16 [512, 4096], P('dp', 'mp'), as said below
- pair_block: int32 [8, 8], P(None, 'dp'), may hold values from 0 to 3
- positives: int32 [1536], P('dp'), may hold values from 0 to 127
Outputs:
- loss: float32 [], replicated
- query_grad: float32 [1536, 4096], P('dp', 'mp')
- passage_grad: float32 [512, 4096], P('dp', 'mp')
The draws below stay inside these ranges and needn't reach their ends.
Inputs may be any that keep to these rules, and one draw needn't show every extreme that they name: `queries`: query embeddings. `passages`: passage embeddings.
All inputs are finite; a program needn't handle non-finite values.
Results may differ from the reference program's by a relative error of at most 0.0019.
Values may be sent and summed in bfloat16 or wider, within the bound.
A program may use at most 64 MiB of HBM per device.

```python
import math
import jax
import jax.numpy as jnp
import numpy as np
from jax import lax

D = 4096
QBLK = 192
PBLK = 16
PB_DEV = 4
QUERIES = 1536
PASSAGES = 512
CANDS = 128
N_DP = 8


def draw_queries(key, part):
    key = jax.random.fold_in(key, 3)
    first = jax.random.fold_in(key, 0)
    values = 0.177 * jax.random.normal(first, (QUERIES, D), jnp.float32)
    return values.astype(jnp.bfloat16)


def draw_passages(key, part):
    key = jax.random.fold_in(key, 5)
    first = jax.random.fold_in(key, 0)
    values = 0.177 * jax.random.normal(first, (PASSAGES, D), jnp.float32)
    return values.astype(jnp.bfloat16)


def set_ends(entries, rng, low, largest):
    spot = [jax.random.randint(jax.random.fold_in(rng, axis), (), 0, length) for axis, length in enumerate(entries.shape)]
    widest = entries.shape.index(max(entries.shape))
    neighbour = spot[:widest] + [(spot[widest] + 1) % entries.shape[widest]] + spot[widest + 1:]
    return entries.at[tuple(spot)].set(low).at[tuple(neighbour)].set(largest)


def cumulative_ranks(amount, slope):
    loads = [(1 << 20) // math.isqrt(rank ** slope) + 1 for rank in range(1, amount + 1)]
    width = 1 + sum(loads) // (1 << 30)
    return np.cumsum(np.array([max(1, weight // width) for weight in loads]))


def ranked(own_key, dims, amount, slope):
    listing = cumulative_ranks(amount, slope)
    pick = jax.random.randint(jax.random.fold_in(own_key, 1), dims, 0, int(listing[amount - 1]))
    standing = jnp.searchsorted(jnp.asarray(listing, jnp.int32), pick, side="right")
    return jax.random.permutation(jax.random.fold_in(own_key, 2), amount)[standing].astype(jnp.int32)


def setup_inputs(seed: int = 0) -> dict:
    key_of = jax.random.split(jax.random.key(seed), 5)
    queries = draw_queries(jax.random.fold_in(key_of[4], 71), 0)
    passages = draw_passages(jax.random.fold_in(key_of[4], 71), 0)
    pair_block = set_ends(ranked(key_of[2], (N_DP, N_DP), PB_DEV, 2), jax.random.fold_in(key_of[2], 3), 0, PB_DEV - 1).astype(jnp.int32)
    positives = set_ends(jax.random.randint(key_of[3], (QUERIES,), 0, CANDS), jax.random.fold_in(key_of[3], 1), 0, CANDS - 1).astype(jnp.int32)
    return dict(queries=queries, passages=passages, pair_block=pair_block, positives=positives)


def weigh(scores, picks):
    top = jnp.max(scores, axis=1, keepdims=True)
    shifted = jnp.exp(scores - top)
    total = jnp.sum(shifted, axis=1, keepdims=True)
    probs = shifted / total
    hits = picks[:, None] == lax.broadcasted_iota(jnp.int32, scores.shape, 1)
    chosen = jnp.sum(jnp.where(hits, scores, 0.0), axis=1)
    losses = top[:, 0] + jnp.log(total[:, 0]) - chosen
    weights = (probs - hits.astype(scores.dtype)).astype(jnp.bfloat16)
    return weights, jnp.sum(losses)


def reference(queries, passages, pair_block, positives):
    groups = jnp.arange(N_DP, dtype=jnp.int32)[None, :] * (PB_DEV * PBLK)
    starts = groups + pair_block.astype(jnp.int32) * PBLK
    inner = jnp.arange(PBLK, dtype=jnp.int32)[None, None, :]
    rows = (starts[:, :, None] + inner).reshape(N_DP, CANDS).astype(jnp.int32)

    def step(grads, inputs):
        block_q, index, picks = inputs
        cands = passages[index]
        scores = jnp.dot(block_q, cands.T, preferred_element_type=jnp.float32)
        weights, loss_sum = weigh(scores, picks)
        query_part = jnp.dot(weights, cands, preferred_element_type=jnp.float32)
        cand_grad = jnp.dot(weights.T, block_q, preferred_element_type=jnp.float32)
        grads = grads.at[index].add(cand_grad)
        return grads, (query_part, loss_sum)

    start = jnp.zeros((PASSAGES, D), jnp.float32)
    grads, (query_parts, loss_sums) = lax.scan(
        step, start,
        (queries.reshape(N_DP, QBLK, D), rows, positives.reshape(N_DP, QBLK)))
    loss = jnp.sum(loss_sums) / QUERIES
    return loss, query_parts.reshape(QUERIES, D), grads
```

```python
import functools
import jax
import jax.numpy as jnp
from jax import lax
from jax.experimental import pallas as pl
from jax.experimental.pallas import tpu as pltpu
from jax.sharding import PartitionSpec as P

PBLK = 16
PB_DEV = 4
MESH = pl.DeviceIdType.MESH
UNROLL = 8


def flip(index, step, count):
    result, bit = 0, 1
    while bit < count:
        mine, other = (index // bit) % 2, (step // bit) % 2
        result = result + bit * (mine + other - 2 * mine * other)
        bit *= 2
    return result


def each(low, high, body):
    if high - low <= UNROLL:
        for step in range(low, high):
            body(step)
    else:
        lax.fori_loop(low, high, lambda step, carry: (body(step), carry)[1], 0)


def kernel(
    n, m, q_hbm, p_hbm, pair_ref, pos_ref, loss_ref, qgrad_ref, pgrad_ref,
    q, p, outgoing, flat, part, shares, weights, turned, hits,
    sent_wide, sent_slim, got_wide, got_slim, loss_mp, loss_dp,
    local_sem, a_send, a_recv, b_send, b_recv, c_send, c_recv,
    d_send, d_recv, e_send, e_recv, f_send, f_recv,
):
    half = n // 2
    rows = q.shape[0]
    share = rows // m
    me = lax.axis_index("dp")
    mine = lax.axis_index("mp")

    def remote(src, dst, send, recv, device):
        return pltpu.make_async_remote_copy(
            src_ref=src, dst_ref=dst, send_sem=send, recv_sem=recv,
            device_id=device, device_id_type=MESH,
        )

    def across(step):
        return (flip(me, step, n), mine)

    def beside(step):
        return (me, flip(mine, step, m))

    load_p = pltpu.make_async_copy(p_hbm, p, local_sem.at[0])
    load_q = pltpu.make_async_copy(q_hbm, q, local_sem.at[1])
    load_p.start()
    load_q.start()
    barrier = pltpu.get_barrier_semaphore()

    def greet(step):
        pl.semaphore_signal(barrier, inc=1, device_id=across(step), device_id_type=MESH)

    each(1, n, greet)
    for step in range(1, m):
        pl.semaphore_signal(barrier, inc=1, device_id=beside(step), device_id_type=MESH)

    def slot(step):
        return pl.ds(step * PBLK, PBLK)

    def chosen(step):
        return p[pair_ref[flip(me, step, n), 0]]

    load_p.wait()

    def pack(step):
        outgoing[step] = chosen(step)

    each(1, n, pack)
    flat[0:PBLK, :] = chosen(0)
    pl.semaphore_wait(barrier, n - 1 + m - 1)

    def passage(step):
        return remote(
            outgoing.at[step], flat.at[slot(step)], a_send.at[step], a_recv.at[step], across(step)
        )

    each(half, n, lambda step: passage(step).start())
    each(1, half, lambda step: passage(step).start())

    lanes = lax.broadcasted_iota(jnp.int32, (1, n * PBLK), 1)
    first = pl.multiple_of(mine * share, share)

    def mark(row):
        spot = pos_ref[first + row] ^ (me * PBLK)
        hits[pl.ds(row, 1), :] = (lanes == spot).astype(jnp.float32)

    for row in range(share):
        mark(row)
    load_q.wait()
    each(1, n, lambda step: passage(step).wait_recv())

    part[...] = lax.dot_general(
        q[...], flat[...], (((1,), (1,)), ((), ())), preferred_element_type=jnp.float32
    )

    def their_rows(step):
        return pl.ds(pl.multiple_of(flip(mine, step, m) * share, share), share)

    def score(step):
        return remote(
            part.at[their_rows(step)], shares.at[step], b_send.at[step], b_recv.at[step],
            beside(step),
        )

    for step in reversed(range(1, m)):
        score(step).start()
    scores = part[pl.ds(first, share), :]
    for step in range(1, m):
        score(step).wait_recv()
        scores = scores + shares[step]
    top = jnp.max(scores, axis=1, keepdims=True)
    shifted = jnp.exp(scores - top)
    total = jnp.sum(shifted, axis=1, keepdims=True)
    hit = hits[...]
    weights[pl.ds(first, share), :] = (shifted / total - hit).astype(jnp.bfloat16)

    def weight(step):
        place = pl.ds(first, share)
        return remote(
            weights.at[place], weights.at[place], c_send.at[step], c_recv.at[step], beside(step)
        )

    def arriving(step):
        place = their_rows(step)
        return remote(
            weights.at[place], weights.at[place], c_send.at[step], c_recv.at[step], beside(step)
        )

    for step in reversed(range(1, m)):
        weight(step).start()

    positive = jnp.sum(hit * scores, axis=1, keepdims=True)
    losses = top + jnp.log(total) - positive
    loss_mp[0] = jnp.broadcast_to(jnp.sum(losses, axis=0, keepdims=True), loss_mp.shape[1:])

    def loss_beside(step):
        return remote(
            loss_mp.at[0], loss_mp.at[step], d_send.at[step], d_recv.at[step], beside(step)
        )

    for step in range(1, m):
        loss_beside(step).start()
    for step in range(1, m):
        arriving(step).wait_recv()
    turned[...] = weights[...].astype(jnp.float32).T.astype(jnp.bfloat16)

    def slim(step):
        return remote(
            sent_slim.at[step - half], got_slim.at[step - half], e_send.at[step], e_recv.at[step],
            across(step),
        )

    def wide(step):
        return remote(
            sent_wide.at[step], got_wide.at[step], e_send.at[step], e_recv.at[step], across(step)
        )

    group = min(half, 4)

    def grads(index):
        block = turned[pl.ds(index * group * PBLK, group * PBLK), :]
        result = jnp.dot(block, q[...], preferred_element_type=jnp.float32)
        return result.reshape(group, PBLK, q.shape[1])

    def give_slim(index):
        sent_slim[pl.ds(index * group - half, group)] = grads(index).astype(jnp.bfloat16)
        for place in range(group):
            slim(index * group + place).start()

    def give_wide(index):
        sent_wide[pl.ds(index * group, group)] = grads(index)
        for place in range(group):
            step = index * group + place
            if isinstance(step, int):
                if step:
                    wide(step).start()
            else:
                pl.when(step > 0)(lambda step=step: wide(step).start())

    each(half // group, n // group, give_slim)
    each(0, half // group, give_wide)

    for step in range(1, m):
        loss_beside(step).wait_recv()
    loss_dp[0] = jnp.sum(loss_mp[...], axis=0)

    def loss_across(step):
        return remote(
            loss_dp.at[0], loss_dp.at[step], f_send.at[step], f_recv.at[step], across(step)
        )

    each(1, n, lambda step: loss_across(step).start())

    qgrad_ref[...] = jnp.dot(weights[...], flat[...], preferred_element_type=jnp.float32)

    pgrad_ref[...] = jnp.zeros_like(pgrad_ref)

    def collect(step, block):
        pick = jnp.full(block.shape, pair_ref[flip(me, step, n), 0], jnp.int32)
        for place in range(PB_DEV):
            pgrad_ref[pl.ds(place * PBLK, PBLK), :] += jnp.where(pick == place, block, 0.0)

    def take_wide(step):
        wide(step).wait_recv()
        collect(step, got_wide[step])

    def take_slim(step):
        slim(step).wait_recv()
        collect(step, got_slim[step - half].astype(jnp.float32))

    collect(0, sent_wide[0])
    each(1, half, take_wide)
    each(half, n, take_slim)
    each(1, n, lambda step: loss_across(step).wait_recv())
    loss_ref[...] = jnp.sum(loss_dp[...], axis=0)[0:1, 0:1] / (rows * n)

    def settle(step):
        passage(step).wait_send()
        loss_across(step).wait_send()

    each(1, n, settle)
    each(1, half, lambda step: wide(step).wait_send())
    each(half, n, lambda step: slim(step).wait_send())
    for step in range(1, m):
        score(step).wait_send()
        weight(step).wait_send()
        loss_beside(step).wait_send()


def per_device(n, m, queries, passages, pair_block, positives):
    rows, width = queries.shape
    half, share, cands = n // 2, rows // m, n * PBLK
    vmem, sems = pltpu.VMEM, pltpu.SemaphoreType.DMA
    bf16, f32 = jnp.bfloat16, jnp.float32
    scratch = [
        vmem((rows, width), bf16),
        vmem((PB_DEV, PBLK, width), bf16),
        vmem((n, PBLK, width), bf16),
        vmem((cands, width), bf16),
        vmem((rows, cands), f32),
        vmem((m, share, cands), f32),
        vmem((rows, cands), bf16),
        vmem((cands, rows), bf16),
        vmem((share, cands), f32),
        vmem((half, PBLK, width), f32),
        vmem((half, PBLK, width), bf16),
        vmem((half, PBLK, width), f32),
        vmem((half, PBLK, width), bf16),
        vmem((m, 8, 128), f32),
        vmem((n, 8, 128), f32),
        sems((2,)),
        sems((n,)), sems((n,)), sems((m,)), sems((m,)), sems((m,)), sems((m,)),
        sems((m,)), sems((m,)), sems((n,)), sems((n,)), sems((n,)), sems((n,)),
    ]
    anywhere = pl.BlockSpec(memory_space=pl.ANY)
    smem = pl.BlockSpec(memory_space=pltpu.SMEM)
    inside = pl.BlockSpec(memory_space=pltpu.VMEM)
    loss, query_grad, passage_grad = pl.pallas_call(
        functools.partial(kernel, n, m),
        out_shape=[
            jax.ShapeDtypeStruct((1, 1), f32),
            jax.ShapeDtypeStruct((rows, width), f32),
            jax.ShapeDtypeStruct(passages.shape, f32),
        ],
        in_specs=[anywhere, anywhere, smem, smem],
        out_specs=[inside, inside, inside],
        scratch_shapes=scratch,
        compiler_params=pltpu.CompilerParams(
            collective_id=0, has_side_effects=True,
            vmem_limit_bytes=(16 if n <= 16 else 56) << 20,
        ),
    )(queries, passages.reshape(PB_DEV, PBLK, width), pair_block, positives)
    return loss.reshape(()), query_grad, passage_grad


def solution(mesh):
    n, m = mesh.shape["dp"], mesh.shape["mp"]
    in_specs = (P("dp", "mp"), P("dp", "mp"), P(None, "dp"), P("dp"))
    out_specs = (P(), P("dp", "mp"), P("dp", "mp"))
    return jax.shard_map(
        functools.partial(per_device, n, m),
        mesh=mesh, in_specs=in_specs, out_specs=out_specs, check_vma=False,
    )
```

```python
import functools
import jax
import jax.numpy as jnp
from jax import lax
from jax.experimental import pallas as pl
from jax.experimental.pallas import tpu as pltpu
from jax.sharding import PartitionSpec as P

PBLK = 16
PB_DEV = 4
MESH = pl.DeviceIdType.MESH
UNROLL = 8


def flip(index, step, count):
    result, bit = 0, 1
    while bit < count:
        mine, other = (index // bit) % 2, (step // bit) % 2
        result = result + bit * (mine + other - 2 * mine * other)
        bit *= 2
    return result


def each(low, high, body):
    if high - low <= UNROLL:
        for step in range(low, high):
            body(step)
    else:
        lax.fori_loop(low, high, lambda step, carry: (body(step), carry)[1], 0)


def kernel(
    n, m, q_hbm, p_hbm, pair_ref, pos_ref, loss_hbm, qgrad_hbm, pgrad_hbm,
    loss_ref, qgrad_ref, pgrad_ref, q, p, outgoing, flat, part, shares, weights, turned, hits,
    sent_wide, sent_slim, got_wide, got_slim, loss_mp, loss_dp,
    local_sem, a_send, a_recv, b_send, b_recv, c_send, c_recv,
    d_send, d_recv, e_send, e_recv, f_send, f_recv,
):
    half = n // 2
    rows = q.shape[0]
    share = rows // m
    me = lax.axis_index("dp")
    mine = lax.axis_index("mp")

    def remote(src, dst, send, recv, device):
        return pltpu.make_async_remote_copy(
            src_ref=src, dst_ref=dst, send_sem=send, recv_sem=recv,
            device_id=device, device_id_type=MESH,
        )

    def across(step):
        return (flip(me, step, n), mine)

    def beside(step):
        return (me, flip(mine, step, m))

    load_p = pltpu.make_async_copy(p_hbm, p, local_sem.at[0])
    load_q = pltpu.make_async_copy(q_hbm, q, local_sem.at[1])
    load_p.start()
    load_q.start()
    barrier = pltpu.get_barrier_semaphore()

    def greet(step):
        pl.semaphore_signal(barrier, inc=1, device_id=across(step), device_id_type=MESH)

    each(1, n, greet)
    for step in range(1, m):
        pl.semaphore_signal(barrier, inc=1, device_id=beside(step), device_id_type=MESH)

    def slot(step):
        return pl.ds(step * PBLK, PBLK)

    def chosen(step):
        return p[pair_ref[flip(me, step, n)]]

    load_p.wait()

    def pack(step):
        outgoing[step] = chosen(step)

    each(1, n, pack)
    flat[0:PBLK, :] = chosen(0)
    pl.semaphore_wait(barrier, n - 1 + m - 1)

    def passage(step):
        return remote(
            outgoing.at[step], flat.at[slot(step)], a_send.at[step], a_recv.at[step], across(step)
        )

    each(half, n, lambda step: passage(step).start())
    each(1, half, lambda step: passage(step).start())

    lanes = lax.broadcasted_iota(jnp.int32, (1, n * PBLK), 1)
    first = pl.multiple_of(mine * share, share)

    def mark(row):
        spot = pos_ref[first + row] ^ (me * PBLK)
        hits[pl.ds(row, 1), :] = (lanes == spot).astype(jnp.float32)

    for row in range(share):
        mark(row)
    load_q.wait()
    each(1, n, lambda step: passage(step).wait_recv())

    part[...] = lax.dot_general(
        q[...], flat[...], (((1,), (1,)), ((), ())), preferred_element_type=jnp.float32
    )

    def their_rows(step):
        return pl.ds(pl.multiple_of(flip(mine, step, m) * share, share), share)

    def score(step):
        return remote(
            part.at[their_rows(step)], shares.at[step], b_send.at[step], b_recv.at[step],
            beside(step),
        )

    for step in reversed(range(1, m)):
        score(step).start()
    scores = part[pl.ds(first, share), :]
    for step in range(1, m):
        score(step).wait_recv()
        scores = scores + shares[step]
    top = jnp.max(scores, axis=1, keepdims=True)
    shifted = jnp.exp(scores - top)
    total = jnp.sum(shifted, axis=1, keepdims=True)
    hit = hits[...]
    weights[pl.ds(first, share), :] = (shifted / total - hit).astype(jnp.bfloat16)

    def weight(step):
        place = pl.ds(first, share)
        return remote(
            weights.at[place], weights.at[place], c_send.at[step], c_recv.at[step], beside(step)
        )

    def arriving(step):
        place = their_rows(step)
        return remote(
            weights.at[place], weights.at[place], c_send.at[step], c_recv.at[step], beside(step)
        )

    for step in reversed(range(1, m)):
        weight(step).start()

    positive = jnp.sum(hit * scores, axis=1, keepdims=True)
    losses = top + jnp.log(total) - positive
    loss_mp[0] = jnp.broadcast_to(jnp.sum(losses, axis=0, keepdims=True), loss_mp.shape[1:])

    def loss_beside(step):
        return remote(
            loss_mp.at[0], loss_mp.at[step], d_send.at[step], d_recv.at[step], beside(step)
        )

    for step in range(1, m):
        loss_beside(step).start()
    for step in range(1, m):
        arriving(step).wait_recv()
    turned[...] = weights[...].astype(jnp.float32).T.astype(jnp.bfloat16)

    def slim(step):
        return remote(
            sent_slim.at[step - half], got_slim.at[step - half], e_send.at[step], e_recv.at[step],
            across(step),
        )

    def wide(step):
        return remote(
            sent_wide.at[step], got_wide.at[step], e_send.at[step], e_recv.at[step], across(step)
        )

    group = min(half, 4)

    def grads(index):
        block = turned[pl.ds(index * group * PBLK, group * PBLK), :]
        result = jnp.dot(block, q[...], preferred_element_type=jnp.float32)
        return result.reshape(group, PBLK, q.shape[1])

    def give_slim(index):
        sent_slim[pl.ds(index * group - half, group)] = grads(index).astype(jnp.bfloat16)
        for place in range(group):
            slim(index * group + place).start()

    def give_wide(index):
        sent_wide[pl.ds(index * group, group)] = grads(index)
        for place in range(group):
            step = index * group + place
            if isinstance(step, int):
                if step:
                    wide(step).start()
            else:
                pl.when(step > 0)(lambda step=step: wide(step).start())

    each(half // group, n // group, give_slim)
    each(0, half // group, give_wide)

    for step in range(1, m):
        loss_beside(step).wait_recv()
    loss_dp[0] = jnp.sum(loss_mp[...], axis=0)

    def loss_across(step):
        return remote(
            loss_dp.at[0], loss_dp.at[step], f_send.at[step], f_recv.at[step], across(step)
        )

    each(1, n, lambda step: loss_across(step).start())

    qgrad_ref[...] = jnp.dot(weights[...], flat[...], preferred_element_type=jnp.float32)
    save_q = pltpu.make_async_copy(qgrad_ref, qgrad_hbm, local_sem.at[2])
    save_q.start()

    pgrad_ref[...] = jnp.zeros_like(pgrad_ref)

    def collect(step, block):
        pick = jnp.full(block.shape, pair_ref[flip(me, step, n)], jnp.int32)
        for place in range(PB_DEV):
            pgrad_ref[pl.ds(place * PBLK, PBLK), :] += jnp.where(pick == place, block, 0.0)

    def take_wide(step):
        wide(step).wait_recv()
        collect(step, got_wide[step])

    def take_slim(step):
        slim(step).wait_recv()
        collect(step, got_slim[step - half].astype(jnp.float32))

    collect(0, sent_wide[0])
    each(1, half, take_wide)
    each(half, n, take_slim)
    save_p = pltpu.make_async_copy(pgrad_ref, pgrad_hbm, local_sem.at[3])
    save_p.start()
    each(1, n, lambda step: loss_across(step).wait_recv())
    loss_ref[...] = jnp.sum(loss_dp[...], axis=0)[0:1, 0:1] / (rows * n)
    save_loss = pltpu.make_async_copy(loss_ref, loss_hbm, local_sem.at[4])
    save_loss.start()

    def settle(step):
        passage(step).wait_send()
        loss_across(step).wait_send()

    each(1, n, settle)
    each(1, half, lambda step: wide(step).wait_send())
    each(half, n, lambda step: slim(step).wait_send())
    for step in range(1, m):
        score(step).wait_send()
        weight(step).wait_send()
        loss_beside(step).wait_send()
    save_q.wait()
    save_p.wait()
    save_loss.wait()


def hand_over(*refs):
    sems = refs[-1]
    count = len(refs) // 2
    copies = [
        pltpu.make_async_copy(refs[place], refs[count + place], sems.at[place])
        for place in range(count)
    ]
    for copy in copies:
        copy.start()
    for copy in copies:
        copy.wait()


def per_device(n, m, queries, passages, pair_block, positives):
    rows, width = queries.shape
    half, share, cands = n // 2, rows // m, n * PBLK
    vmem, sems = pltpu.VMEM, pltpu.SemaphoreType.DMA
    bf16, f32 = jnp.bfloat16, jnp.float32
    results = [
        jax.ShapeDtypeStruct((1, 1), f32),
        jax.ShapeDtypeStruct((rows, width), f32),
        jax.ShapeDtypeStruct(passages.shape, f32),
    ]
    scratch = [
        vmem((1, 1), f32),
        vmem((rows, width), f32),
        vmem(passages.shape, f32),
        vmem((rows, width), bf16),
        vmem((PB_DEV, PBLK, width), bf16),
        vmem((n, PBLK, width), bf16),
        vmem((cands, width), bf16),
        vmem((rows, cands), f32),
        vmem((m, share, cands), f32),
        vmem((rows, cands), bf16),
        vmem((cands, rows), bf16),
        vmem((share, cands), f32),
        vmem((half, PBLK, width), f32),
        vmem((half, PBLK, width), bf16),
        vmem((half, PBLK, width), f32),
        vmem((half, PBLK, width), bf16),
        vmem((m, 8, 128), f32),
        vmem((n, 8, 128), f32),
        sems((5,)),
        sems((n,)), sems((n,)), sems((m,)), sems((m,)), sems((m,)), sems((m,)),
        sems((m,)), sems((m,)), sems((n,)), sems((n,)), sems((n,)), sems((n,)),
    ]
    anywhere = pl.BlockSpec(memory_space=pl.ANY)
    smem = pl.BlockSpec(memory_space=pltpu.SMEM)
    found = pl.pallas_call(
        functools.partial(kernel, n, m),
        out_shape=results,
        in_specs=[anywhere, anywhere, smem, smem],
        out_specs=[anywhere] * 3,
        scratch_shapes=scratch,
        compiler_params=pltpu.CompilerParams(
            collective_id=0, has_side_effects=True, vmem_limit_bytes=60 << 20,
        ),
    )(queries, passages.reshape(PB_DEV, PBLK, width), pair_block.reshape(n), positives)
    loss, query_grad, passage_grad = pl.pallas_call(
        hand_over,
        out_shape=results,
        in_specs=[anywhere] * 3,
        out_specs=[anywhere] * 3,
        scratch_shapes=[sems((3,))],
        compiler_params=pltpu.CompilerParams(vmem_limit_bytes=60 << 20),
    )(*found)
    return loss.reshape(()), query_grad, passage_grad


def solution(mesh):
    n, m = mesh.shape["dp"], mesh.shape["mp"]
    in_specs = (P("dp", "mp"), P("dp", "mp"), P(None, "dp"), P("dp"))
    out_specs = (P(), P("dp", "mp"), P("dp", "mp"))
    return jax.shard_map(
        functools.partial(per_device, n, m),
        mesh=mesh, in_specs=in_specs, out_specs=out_specs, check_vma=False,
    )
```

```python
import functools
import jax
import jax.numpy as jnp
from jax import lax
from jax.experimental import pallas as pl
from jax.experimental.pallas import tpu as pltpu
from jax.sharding import PartitionSpec as P

PBLK = 16
PB_DEV = 4
MESH = pl.DeviceIdType.MESH
UNROLL = 8


def flip(index, step, count):
    result, bit = 0, 1
    while bit < count:
        mine, other = (index // bit) % 2, (step // bit) % 2
        result = result + bit * (mine + other - 2 * mine * other)
        bit *= 2
    return result


def each(low, high, body):
    if high - low <= UNROLL:
        for step in range(low, high):
            body(step)
    else:
        lax.fori_loop(low, high, lambda step, carry: (body(step), carry)[1], 0)


def kernel(
    n, m, q_hbm, p_hbm, pair_hbm, pos_hbm, loss_hbm, qgrad_hbm, pgrad_hbm,
    loss_ref, qgrad_ref, pgrad_ref, pair_ref, pos_ref, q, p, outgoing, flat, part, shares, weights, turned, hits,
    sent_wide, sent_slim, got_wide, got_slim, loss_mp, loss_dp,
    local_sem, a_send, a_recv, b_send, b_recv, c_send, c_recv,
    d_send, d_recv, e_send, e_recv, f_send, f_recv,
):
    half = n // 2
    rows = q.shape[0]
    share = rows // m
    me = lax.axis_index("dp")
    mine = lax.axis_index("mp")

    def remote(src, dst, send, recv, device):
        return pltpu.make_async_remote_copy(
            src_ref=src, dst_ref=dst, send_sem=send, recv_sem=recv,
            device_id=device, device_id_type=MESH,
        )

    def across(step):
        return (flip(me, step, n), mine)

    def beside(step):
        return (me, flip(mine, step, m))

    load_p = pltpu.make_async_copy(p_hbm, p, local_sem.at[0])
    load_q = pltpu.make_async_copy(q_hbm, q, local_sem.at[1])
    load_pair = pltpu.make_async_copy(pair_hbm, pair_ref, local_sem.at[2])
    load_pos = pltpu.make_async_copy(pos_hbm, pos_ref, local_sem.at[3])
    load_pair.start()
    load_p.start()
    load_pos.start()
    load_q.start()
    barrier = pltpu.get_barrier_semaphore()

    def greet(step):
        pl.semaphore_signal(barrier, inc=1, device_id=across(step), device_id_type=MESH)

    each(1, n, greet)
    for step in range(1, m):
        pl.semaphore_signal(barrier, inc=1, device_id=beside(step), device_id_type=MESH)

    def slot(step):
        return pl.ds(step * PBLK, PBLK)

    def chosen(step):
        return p[pair_ref[flip(me, step, n)]]

    load_pair.wait()
    load_p.wait()

    def pack(step):
        outgoing[step] = chosen(step)

    each(1, n, pack)
    flat[0:PBLK, :] = chosen(0)
    pl.semaphore_wait(barrier, n - 1 + m - 1)

    def passage(step):
        return remote(
            outgoing.at[step], flat.at[slot(step)], a_send.at[step], a_recv.at[step], across(step)
        )

    each(half, n, lambda step: passage(step).start())
    each(1, half, lambda step: passage(step).start())

    lanes = lax.broadcasted_iota(jnp.int32, (1, n * PBLK), 1)
    first = pl.multiple_of(mine * share, share)

    def mark(row):
        spot = pos_ref[first + row] ^ (me * PBLK)
        hits[pl.ds(row, 1), :] = (lanes == spot).astype(jnp.float32)

    load_pos.wait()
    for row in range(share):
        mark(row)
    load_q.wait()
    each(1, n, lambda step: passage(step).wait_recv())

    part[...] = lax.dot_general(
        q[...], flat[...], (((1,), (1,)), ((), ())), preferred_element_type=jnp.float32
    )

    def their_rows(step):
        return pl.ds(pl.multiple_of(flip(mine, step, m) * share, share), share)

    def score(step):
        return remote(
            part.at[their_rows(step)], shares.at[step], b_send.at[step], b_recv.at[step],
            beside(step),
        )

    for step in reversed(range(1, m)):
        score(step).start()
    scores = part[pl.ds(first, share), :]
    for step in range(1, m):
        score(step).wait_recv()
        scores = scores + shares[step]
    top = jnp.max(scores, axis=1, keepdims=True)
    shifted = jnp.exp(scores - top)
    total = jnp.sum(shifted, axis=1, keepdims=True)
    hit = hits[...]
    weights[pl.ds(first, share), :] = (shifted / total - hit).astype(jnp.bfloat16)

    def weight(step):
        place = pl.ds(first, share)
        return remote(
            weights.at[place], weights.at[place], c_send.at[step], c_recv.at[step], beside(step)
        )

    def arriving(step):
        place = their_rows(step)
        return remote(
            weights.at[place], weights.at[place], c_send.at[step], c_recv.at[step], beside(step)
        )

    for step in reversed(range(1, m)):
        weight(step).start()

    positive = jnp.sum(hit * scores, axis=1, keepdims=True)
    losses = top + jnp.log(total) - positive
    loss_mp[0] = jnp.broadcast_to(jnp.sum(losses, axis=0, keepdims=True), loss_mp.shape[1:])

    def loss_beside(step):
        return remote(
            loss_mp.at[0], loss_mp.at[step], d_send.at[step], d_recv.at[step], beside(step)
        )

    for step in range(1, m):
        loss_beside(step).start()
    for step in range(1, m):
        arriving(step).wait_recv()
    turned[...] = weights[...].astype(jnp.float32).T.astype(jnp.bfloat16)

    def slim(step):
        return remote(
            sent_slim.at[step - half], got_slim.at[step - half], e_send.at[step], e_recv.at[step],
            across(step),
        )

    def wide(step):
        return remote(
            sent_wide.at[step], got_wide.at[step], e_send.at[step], e_recv.at[step], across(step)
        )

    group = min(half, 4)

    def grads(index):
        block = turned[pl.ds(index * group * PBLK, group * PBLK), :]
        result = jnp.dot(block, q[...], preferred_element_type=jnp.float32)
        return result.reshape(group, PBLK, q.shape[1])

    def give_slim(index):
        sent_slim[pl.ds(index * group - half, group)] = grads(index).astype(jnp.bfloat16)
        for place in range(group):
            slim(index * group + place).start()

    def give_wide(index):
        sent_wide[pl.ds(index * group, group)] = grads(index)
        for place in range(group):
            step = index * group + place
            if isinstance(step, int):
                if step:
                    wide(step).start()
            else:
                pl.when(step > 0)(lambda step=step: wide(step).start())

    each(half // group, n // group, give_slim)
    each(0, half // group, give_wide)

    for step in range(1, m):
        loss_beside(step).wait_recv()
    loss_dp[0] = jnp.sum(loss_mp[...], axis=0)

    def loss_across(step):
        return remote(
            loss_dp.at[0], loss_dp.at[step], f_send.at[step], f_recv.at[step], across(step)
        )

    each(1, n, lambda step: loss_across(step).start())

    qgrad_ref[...] = jnp.dot(weights[...], flat[...], preferred_element_type=jnp.float32)
    save_q = pltpu.make_async_copy(qgrad_ref, qgrad_hbm, local_sem.at[4])
    save_q.start()

    pgrad_ref[...] = jnp.zeros_like(pgrad_ref)

    def collect(step, block):
        pick = jnp.full(block.shape, pair_ref[flip(me, step, n)], jnp.int32)
        for place in range(PB_DEV):
            pgrad_ref[pl.ds(place * PBLK, PBLK), :] += jnp.where(pick == place, block, 0.0)

    def take_wide(step):
        wide(step).wait_recv()
        collect(step, got_wide[step])

    def take_slim(step):
        slim(step).wait_recv()
        collect(step, got_slim[step - half].astype(jnp.float32))

    collect(0, sent_wide[0])
    each(1, half, take_wide)
    each(half, n, take_slim)
    save_p = pltpu.make_async_copy(pgrad_ref, pgrad_hbm, local_sem.at[5])
    save_p.start()
    each(1, n, lambda step: loss_across(step).wait_recv())
    loss_ref[...] = jnp.sum(loss_dp[...], axis=0)[0:1, 0:1] / (rows * n)
    save_loss = pltpu.make_async_copy(loss_ref, loss_hbm, local_sem.at[6])
    save_loss.start()

    def settle(step):
        passage(step).wait_send()
        loss_across(step).wait_send()

    each(1, n, settle)
    each(1, half, lambda step: wide(step).wait_send())
    each(half, n, lambda step: slim(step).wait_send())
    for step in range(1, m):
        score(step).wait_send()
        weight(step).wait_send()
        loss_beside(step).wait_send()
    save_q.wait()
    save_p.wait()
    save_loss.wait()


def hand_over(loss_in, qgrad_in, pgrad_in, loss_out, qgrad_out, pgrad_out, loss, qgrad, pgrad, sems):
    parts = [(loss_in, loss, loss_out)]
    piece = 64
    for source, held, target in ((qgrad_in, qgrad, qgrad_out), (pgrad_in, pgrad, pgrad_out)):
        for start in range(0, held.shape[0], piece):
            place = pl.ds(start, piece)
            parts.append((source.at[place], held.at[place], target.at[place]))
    loads, stores = [], []
    for index, (source, held, target) in enumerate(parts):
        loads.append(pltpu.make_async_copy(source, held, sems.at[0, index]))
        stores.append(pltpu.make_async_copy(held, target, sems.at[1, index]))
    for load in loads:
        load.start()
    for load, store in zip(loads, stores):
        load.wait()
        store.start()
    for store in stores:
        store.wait()


def per_device(n, m, queries, passages, pair_block, positives):
    rows, width = queries.shape
    half, share, cands = n // 2, rows // m, n * PBLK
    vmem, sems = pltpu.VMEM, pltpu.SemaphoreType.DMA
    bf16, f32 = jnp.bfloat16, jnp.float32
    results = [
        jax.ShapeDtypeStruct((1, 1), f32),
        jax.ShapeDtypeStruct((rows, width), f32),
        jax.ShapeDtypeStruct(passages.shape, f32),
    ]
    held = [vmem((1, 1), f32), vmem((rows, width), f32), vmem(passages.shape, f32)]
    scratch = held + [
        pltpu.SMEM((n,), jnp.int32),
        pltpu.SMEM((rows,), jnp.int32),
        vmem((rows, width), bf16),
        vmem((PB_DEV, PBLK, width), bf16),
        vmem((n, PBLK, width), bf16),
        vmem((cands, width), bf16),
        vmem((rows, cands), f32),
        vmem((m, share, cands), f32),
        vmem((rows, cands), bf16),
        vmem((cands, rows), bf16),
        vmem((share, cands), f32),
        vmem((half, PBLK, width), f32),
        vmem((half, PBLK, width), bf16),
        vmem((half, PBLK, width), f32),
        vmem((half, PBLK, width), bf16),
        vmem((m, 8, 128), f32),
        vmem((n, 8, 128), f32),
        sems((7,)),
        sems((n,)), sems((n,)), sems((m,)), sems((m,)), sems((m,)), sems((m,)),
        sems((m,)), sems((m,)), sems((n,)), sems((n,)), sems((n,)), sems((n,)),
    ]
    anywhere = pl.BlockSpec(memory_space=pl.ANY)
    found = pl.pallas_call(
        functools.partial(kernel, n, m),
        out_shape=results,
        in_specs=[anywhere] * 4,
        out_specs=[anywhere] * 3,
        scratch_shapes=scratch,
        compiler_params=pltpu.CompilerParams(
            collective_id=0, has_side_effects=True,
            vmem_limit_bytes=60 << 20,
        ),
    )(queries, passages.reshape(PB_DEV, PBLK, width), pair_block.reshape(n), positives)
    loss, query_grad, passage_grad = pl.pallas_call(
        hand_over,
        out_shape=results,
        in_specs=[anywhere] * 3,
        out_specs=[anywhere] * 3,
        scratch_shapes=held + [sems((2, 1 + (rows + passages.shape[0]) // 64))],
        compiler_params=pltpu.CompilerParams(vmem_limit_bytes=60 << 20),
    )(*found)
    return loss.reshape(()), query_grad, passage_grad


def solution(mesh):
    n, m = mesh.shape["dp"], mesh.shape["mp"]
    in_specs = (P("dp", "mp"), P("dp", "mp"), P(None, "dp"), P("dp"))
    out_specs = (P(), P("dp", "mp"), P("dp", "mp"))
    return jax.shard_map(
        functools.partial(per_device, n, m),
        mesh=mesh, in_specs=in_specs, out_specs=out_specs, check_vma=False,
    )
```

```python
import functools
import jax
import jax.numpy as jnp
from jax import lax
from jax.experimental import pallas as pl
from jax.experimental.pallas import tpu as pltpu
from jax.sharding import PartitionSpec as P

PBLK = 16
PB_DEV = 4
MESH = pl.DeviceIdType.MESH
UNROLL = 8
LANES = 128


def flip(index, step, count):
    result, bit = 0, 1
    while bit < count:
        mine, other = (index // bit) % 2, (step // bit) % 2
        result = result + bit * (mine + other - 2 * mine * other)
        bit *= 2
    return result


def each(low, high, body):
    if high - low <= UNROLL:
        for step in range(low, high):
            body(step)
    else:
        lax.fori_loop(low, high, lambda step, carry: (body(step), carry)[1], 0)


def kernel(
    n, m, q_hbm, p_hbm, pair_hbm, pos_hbm, loss_hbm, qgrad_hbm, pgrad_hbm,
    loss_ref, qgrad_ref, pgrad_ref, pair_ref, pos_ref, q, p, outgoing, flat, part, shares, turned,
    sent_wide, sent_slim, got_wide, got_slim, loss_dp,
    local_sem, a_send, a_recv, b_send, b_recv, e_send, e_recv, f_send, f_recv,
):
    half = n // 2
    rows = q.shape[0]
    me = lax.axis_index("dp")
    mine = lax.axis_index("mp")

    def remote(src, dst, send, recv, device):
        return pltpu.make_async_remote_copy(
            src_ref=src, dst_ref=dst, send_sem=send, recv_sem=recv,
            device_id=device, device_id_type=MESH,
        )

    def across(step):
        return (flip(me, step, n), mine)

    def beside(step):
        return (me, flip(mine, step, m))

    load_p = pltpu.make_async_copy(p_hbm, p, local_sem.at[0])
    load_q = pltpu.make_async_copy(q_hbm, q, local_sem.at[1])
    load_pair = pltpu.make_async_copy(pair_hbm, pair_ref, local_sem.at[2])
    load_pos = pltpu.make_async_copy(pos_hbm, pos_ref, local_sem.at[3])
    load_pair.start()
    load_p.start()
    load_pos.start()
    load_q.start()
    barrier = pltpu.get_barrier_semaphore()

    def greet(step):
        pl.semaphore_signal(barrier, inc=1, device_id=across(step), device_id_type=MESH)

    each(1, n, greet)
    for step in range(1, m):
        pl.semaphore_signal(barrier, inc=1, device_id=beside(step), device_id_type=MESH)

    def slot(step):
        return pl.ds(step * PBLK, PBLK)

    def chosen(step):
        return p[pair_ref[flip(me, step, n)]]

    load_pair.wait()
    load_p.wait()

    def pack(step):
        outgoing[step] = chosen(step)

    each(1, n, pack)
    flat[0:PBLK, :] = chosen(0)
    pl.semaphore_wait(barrier, n - 1 + m - 1)

    def passage(step):
        return remote(
            outgoing.at[step], flat.at[slot(step)], a_send.at[step], a_recv.at[step], across(step)
        )

    each(half, n, lambda step: passage(step).start())
    each(1, half, lambda step: passage(step).start())

    load_pos.wait()
    load_q.wait()

    chunks = ((0, half), (half, half + n // 4), (half + n // 4, n))

    def packed(index):
        low, high = chunks[index]
        size = (high - low) * PBLK
        return pl.ds(low * PBLK * 3 // 2, size * 3 // 2), size

    def score(index, step):
        place, _ = packed(index)
        return remote(
            part.at[place], shares.at[step, place], b_send.at[index, step],
            b_recv.at[index, step], beside(step),
        )

    for index, (low, high) in enumerate(chunks):
        each(max(low, 1), high, lambda step: passage(step).wait_recv())
        block = lax.dot_general(
            flat[low * PBLK:high * PBLK, :], q[...], (((1,), (1,)), ((), ())),
            preferred_element_type=jnp.float32,
        )
        place, size = packed(index)
        part[pl.ds(place.start, size), :] = block[:, :LANES]
        part[pl.ds(place.start + size, size // 2), :] = jnp.concatenate(
            [block[:size // 2, LANES:], block[size // 2:, LANES:]], axis=1
        )
        for step in reversed(range(1, m)):
            score(index, step).start()

    def swap(row):
        return jnp.concatenate([row[:, LANES // 2:], row[:, :LANES // 2]], axis=1)

    spots = pos_ref[...] ^ (me * PBLK)
    spots_a = spots[:, :LANES]
    spots_b = jnp.concatenate([spots[:, LANES:], spots[:, LANES:]], axis=1)
    scores_a, scores_b, hits_a, hits_b = [], [], [], []
    for index, (low, high) in enumerate(chunks):
        place, size = packed(index)
        for step in range(1, m):
            score(index, step).wait_recv()
        terms = [part[place, :]] + [shares[step, place, :] for step in range(1, m)]
        while len(terms) > 1:
            terms = [first + second for first, second in zip(terms[::2], terms[1::2])]
        scores_a.append(terms[0][:size])
        scores_b.append(terms[0][size:])
        down = lax.broadcasted_iota(jnp.int32, (size, LANES), 0) + low * PBLK
        hits_a.append(down == spots_a)
        down = lax.broadcasted_iota(jnp.int32, (size // 2, LANES), 0) + low * PBLK
        right = lax.broadcasted_iota(jnp.int32, (size // 2, LANES), 1) // (LANES // 2)
        hits_b.append(down + right * (size // 2) == spots_b)

    def gathered(blocks, combine, reduce):
        return functools.reduce(combine, [reduce(block, axis=0, keepdims=True) for block in blocks])

    def softmax(scores, hits, paired):
        top = gathered(scores, jnp.maximum, jnp.max)
        if paired:
            top = jnp.maximum(top, swap(top))
        raised = [jnp.exp(block - top) for block in scores]
        total = gathered(raised, jnp.add, jnp.sum)
        picked = [jnp.where(hit, block, 0.0) for hit, block in zip(hits, scores)]
        positive = gathered(picked, jnp.add, jnp.sum)
        if paired:
            total = total + swap(total)
            positive = positive + swap(positive)
        inverse = 1.0 / total
        weights = [
            (block * inverse - hit.astype(jnp.float32)).astype(jnp.bfloat16)
            for block, hit in zip(raised, hits)
        ]
        return weights, top + jnp.log(total) - positive

    weights_a, losses_a = softmax(scores_a, hits_a, False)
    weights_b, losses_b = softmax(scores_b, hits_b, True)
    for (low, high), first, second in zip(chunks, weights_a, weights_b):
        start, size = low * PBLK, (high - low) * PBLK
        turned[pl.ds(start, size), pl.ds(0, LANES)] = first
        rest = pl.ds(LANES, LANES // 2)
        turned[pl.ds(start, size // 2), rest] = second[:, :LANES // 2]
        turned[pl.ds(start + size // 2, size // 2), rest] = second[:, LANES // 2:]

    def slim(step):
        return remote(
            sent_slim.at[step - half], got_slim.at[step - half], e_send.at[step], e_recv.at[step],
            across(step),
        )

    def wide(step):
        return remote(
            sent_wide.at[step], got_wide.at[step], e_send.at[step], e_recv.at[step], across(step)
        )

    group = min(half, 4)

    def grads(index):
        block = turned[pl.ds(index * group * PBLK, group * PBLK), :]
        result = jnp.dot(block, q[...], preferred_element_type=jnp.float32)
        return result.reshape(group, PBLK, q.shape[1])

    def give_slim(index):
        sent_slim[pl.ds(index * group - half, group)] = grads(index).astype(jnp.bfloat16)
        for place in range(group):
            slim(index * group + place).start()

    def give_wide(index):
        sent_wide[pl.ds(index * group, group)] = grads(index)
        for place in range(group):
            step = index * group + place
            if isinstance(step, int):
                if step:
                    wide(step).start()
            else:
                pl.when(step > 0)(lambda step=step: wide(step).start())

    each(half // group, n // group, give_slim)
    each(0, half // group, give_wide)

    losses = losses_a + 0.5 * losses_b
    loss_dp[0] = jnp.broadcast_to(jnp.sum(losses, axis=1, keepdims=True), loss_dp.shape[1:])

    def loss_across(step):
        return remote(
            loss_dp.at[0], loss_dp.at[step], f_send.at[step], f_recv.at[step], across(step)
        )

    each(1, n, lambda step: loss_across(step).start())

    qgrad_ref[...] = lax.dot_general(
        turned[...], flat[...], (((0,), (0,)), ((), ())), preferred_element_type=jnp.float32
    )
    save_q = pltpu.make_async_copy(qgrad_ref, qgrad_hbm, local_sem.at[4])
    save_q.start()

    pgrad_ref[...] = jnp.zeros_like(pgrad_ref)

    def collect(step, block):
        pick = jnp.full(block.shape, pair_ref[flip(me, step, n)], jnp.int32)
        for place in range(PB_DEV):
            pgrad_ref[pl.ds(place * PBLK, PBLK), :] += jnp.where(pick == place, block, 0.0)

    def take_wide(step):
        wide(step).wait_recv()
        collect(step, got_wide[step])

    def take_slim(step):
        slim(step).wait_recv()
        collect(step, got_slim[step - half].astype(jnp.float32))

    collect(0, sent_wide[0])
    each(1, half, take_wide)
    each(half, n, take_slim)
    save_p = pltpu.make_async_copy(pgrad_ref, pgrad_hbm, local_sem.at[5])
    save_p.start()
    each(1, n, lambda step: loss_across(step).wait_recv())
    losses = loss_dp[...]
    while losses.shape[0] > 1:
        losses = losses.reshape(losses.shape[0] // 2, 2, *losses.shape[1:])
        losses = losses[:, 0] + losses[:, 1]
    loss_ref[...] = losses[0, 0:1, 0:1] / (rows * n)
    save_loss = pltpu.make_async_copy(loss_ref, loss_hbm, local_sem.at[6])
    save_loss.start()

    def settle(step):
        passage(step).wait_send()
        loss_across(step).wait_send()

    each(1, n, settle)
    each(1, half, lambda step: wide(step).wait_send())
    each(half, n, lambda step: slim(step).wait_send())
    for index in range(len(chunks)):
        for step in range(1, m):
            score(index, step).wait_send()
    save_q.wait()
    save_p.wait()
    save_loss.wait()


def hand_over(loss_in, qgrad_in, pgrad_in, loss_out, qgrad_out, pgrad_out, loss, qgrad, pgrad, sems):
    parts = [(loss_in, loss, loss_out)]
    piece = 64
    for source, held, target in ((qgrad_in, qgrad, qgrad_out), (pgrad_in, pgrad, pgrad_out)):
        for start in range(0, held.shape[0], piece):
            place = pl.ds(start, piece)
            parts.append((source.at[place], held.at[place], target.at[place]))
    loads, stores = [], []
    for index, (source, held, target) in enumerate(parts):
        loads.append(pltpu.make_async_copy(source, held, sems.at[0, index]))
        stores.append(pltpu.make_async_copy(held, target, sems.at[1, index]))
    for load in loads:
        load.start()
    for load, store in zip(loads, stores):
        load.wait()
        store.start()
    for store in stores:
        store.wait()


def per_device(n, m, queries, passages, pair_block, positives):
    rows, width = queries.shape
    half, cands = n // 2, n * PBLK
    vmem, sems = pltpu.VMEM, pltpu.SemaphoreType.DMA
    bf16, f32 = jnp.bfloat16, jnp.float32
    results = [
        jax.ShapeDtypeStruct((1, 1), f32),
        jax.ShapeDtypeStruct((rows, width), f32),
        jax.ShapeDtypeStruct(passages.shape, f32),
    ]
    held = [vmem((1, 1), f32), vmem((rows, width), f32), vmem(passages.shape, f32)]
    scratch = held + [
        pltpu.SMEM((n,), jnp.int32),
        vmem((1, rows), jnp.int32),
        vmem((rows, width), bf16),
        vmem((PB_DEV, PBLK, width), bf16),
        vmem((n, PBLK, width), bf16),
        vmem((cands, width), bf16),
        vmem((cands * 3 // 2, LANES), f32),
        vmem((m, cands * 3 // 2, LANES), f32),
        vmem((cands, rows), bf16),
        vmem((half, PBLK, width), f32),
        vmem((half, PBLK, width), bf16),
        vmem((half, PBLK, width), f32),
        vmem((half, PBLK, width), bf16),
        vmem((n, 8, 128), f32),
        sems((7,)),
        sems((n,)), sems((n,)), sems((3, m)), sems((3, m)),
        sems((n,)), sems((n,)), sems((n,)), sems((n,)),
    ]
    anywhere = pl.BlockSpec(memory_space=pl.ANY)
    found = pl.pallas_call(
        functools.partial(kernel, n, m),
        out_shape=results,
        in_specs=[anywhere] * 4,
        out_specs=[anywhere] * 3,
        scratch_shapes=scratch,
        compiler_params=pltpu.CompilerParams(
            collective_id=0, has_side_effects=True,
            vmem_limit_bytes=60 << 20,
        ),
    )(queries, passages.reshape(PB_DEV, PBLK, width), pair_block.reshape(n),
      positives.reshape(1, rows))
    loss, query_grad, passage_grad = pl.pallas_call(
        hand_over,
        out_shape=results,
        in_specs=[anywhere] * 3,
        out_specs=[anywhere] * 3,
        scratch_shapes=held + [sems((2, 1 + (rows + passages.shape[0]) // 64))],
        compiler_params=pltpu.CompilerParams(vmem_limit_bytes=60 << 20),
    )(*found)
    return loss.reshape(()), query_grad, passage_grad


def solution(mesh):
    n, m = mesh.shape["dp"], mesh.shape["mp"]
    in_specs = (P("dp", "mp"), P("dp", "mp"), P(None, "dp"), P("dp"))
    out_specs = (P(), P("dp", "mp"), P("dp", "mp"))
    return jax.shard_map(
        functools.partial(per_device, n, m),
        mesh=mesh, in_specs=in_specs, out_specs=out_specs, check_vma=False,
    )
```

```python
import functools
import jax
import jax.numpy as jnp
from jax import lax
from jax.experimental import pallas as pl
from jax.experimental.pallas import tpu as pltpu
from jax.sharding import PartitionSpec as P

PBLK = 16
PB_DEV = 4
MESH = pl.DeviceIdType.MESH
UNROLL = 8
LANES = 128


def flip(index, step, count):
    result, bit = 0, 1
    while bit < count:
        mine, other = (index // bit) % 2, (step // bit) % 2
        result = result + bit * (mine + other - 2 * mine * other)
        bit *= 2
    return result


def each(low, high, body):
    if high - low <= UNROLL:
        for step in range(low, high):
            body(step)
    else:
        lax.fori_loop(low, high, lambda step, carry: (body(step), carry)[1], 0)


def kernel(
    n, m, q_hbm, p_hbm, pair_hbm, pos_hbm, loss_hbm, qgrad_hbm, pgrad_hbm,
    loss_ref, qgrad_ref, pgrad_ref, pair_ref, pos_ref, q, p, outgoing, flat, part, shares, turned,
    sent_wide, sent_slim, got_wide, got_slim, loss_dp,
    local_sem, a_send, a_recv, b_send, b_recv, e_send, e_recv, f_send, f_recv,
):
    half = n // 2
    rows = q.shape[0]
    me = lax.axis_index("dp")
    mine = lax.axis_index("mp")

    def remote(src, dst, send, recv, device):
        return pltpu.make_async_remote_copy(
            src_ref=src, dst_ref=dst, send_sem=send, recv_sem=recv,
            device_id=device, device_id_type=MESH,
        )

    def across(step):
        return (flip(me, step, n), mine)

    def beside(step):
        return (me, flip(mine, step, m))

    load_p = pltpu.make_async_copy(p_hbm, p, local_sem.at[0])
    load_q = pltpu.make_async_copy(q_hbm, q, local_sem.at[1])
    load_pair = pltpu.make_async_copy(pair_hbm, pair_ref, local_sem.at[2])
    load_pos = pltpu.make_async_copy(pos_hbm, pos_ref, local_sem.at[3])
    load_pair.start()
    load_p.start()
    load_pos.start()
    load_q.start()
    barrier = pltpu.get_barrier_semaphore()

    def greet(step):
        pl.semaphore_signal(barrier, inc=1, device_id=across(step), device_id_type=MESH)

    each(1, n, greet)
    for step in range(1, m):
        pl.semaphore_signal(barrier, inc=1, device_id=beside(step), device_id_type=MESH)

    def slot(step):
        return pl.ds(step * PBLK, PBLK)

    def chosen(step):
        return p[pair_ref[flip(me, step, n)]]

    load_pair.wait()
    load_p.wait()

    def pack(step):
        outgoing[step] = chosen(step)

    each(1, n, pack)
    flat[0:PBLK, :] = chosen(0)
    pl.semaphore_wait(barrier, n - 1 + m - 1)

    def passage(step):
        return remote(
            outgoing.at[step], flat.at[slot(step)], a_send.at[step], a_recv.at[step], across(step)
        )

    passage(half).start()
    each(1, half, lambda step: passage(step).start())
    each(half + 1, n, lambda step: passage(step).start())

    load_pos.wait()
    load_q.wait()

    chunks = ((0, half), (half, half + n // 4), (half + n // 4, n))

    def packed(index):
        low, high = chunks[index]
        size = (high - low) * PBLK
        return pl.ds(low * PBLK * 3 // 2, size * 3 // 2), size

    def score(index, step):
        place, _ = packed(index)
        return remote(
            part.at[place], shares.at[step, place], b_send.at[index, step],
            b_recv.at[index, step], beside(step),
        )

    for index, (low, high) in enumerate(chunks):
        each(max(low, 1), high, lambda step: passage(step).wait_recv())
        block = lax.dot_general(
            flat[low * PBLK:high * PBLK, :], q[...], (((1,), (1,)), ((), ())),
            preferred_element_type=jnp.float32,
        )
        place, size = packed(index)
        part[pl.ds(place.start, size), :] = block[:, :LANES]
        part[pl.ds(place.start + size, size // 2), :] = jnp.concatenate(
            [block[:size // 2, LANES:], block[size // 2:, LANES:]], axis=1
        )
        for step in reversed(range(1, m)):
            score(index, step).start()

    def swap(row):
        return jnp.concatenate([row[:, LANES // 2:], row[:, :LANES // 2]], axis=1)

    spots = pos_ref[...] ^ (me * PBLK)
    spots_a = spots[:, :LANES]
    spots_b = jnp.concatenate([spots[:, LANES:], spots[:, LANES:]], axis=1)
    scores_a, scores_b, hits_a, hits_b = [], [], [], []
    for index, (low, high) in enumerate(chunks):
        place, size = packed(index)
        for step in range(1, m):
            score(index, step).wait_recv()
        terms = [part[place, :]] + [shares[step, place, :] for step in range(1, m)]
        while len(terms) > 1:
            terms = [first + second for first, second in zip(terms[::2], terms[1::2])]
        scores_a.append(terms[0][:size])
        scores_b.append(terms[0][size:])
        down = lax.broadcasted_iota(jnp.int32, (size, LANES), 0) + low * PBLK
        hits_a.append(down == spots_a)
        down = lax.broadcasted_iota(jnp.int32, (size // 2, LANES), 0) + low * PBLK
        right = lax.broadcasted_iota(jnp.int32, (size // 2, LANES), 1) // (LANES // 2)
        hits_b.append(down + right * (size // 2) == spots_b)

    def gathered(blocks, combine, reduce):
        return functools.reduce(combine, [reduce(block, axis=0, keepdims=True) for block in blocks])

    def softmax(scores, hits, paired):
        top = gathered(scores, jnp.maximum, jnp.max)
        if paired:
            top = jnp.maximum(top, swap(top))
        raised = [jnp.exp(block - top) for block in scores]
        total = gathered(raised, jnp.add, jnp.sum)
        picked = [jnp.where(hit, block, 0.0) for hit, block in zip(hits, scores)]
        positive = gathered(picked, jnp.add, jnp.sum)
        if paired:
            total = total + swap(total)
            positive = positive + swap(positive)
        inverse = 1.0 / total
        weights = [
            (block * inverse - hit.astype(jnp.float32)).astype(jnp.bfloat16)
            for block, hit in zip(raised, hits)
        ]
        return weights, top + jnp.log(total) - positive

    weights_a, losses_a = softmax(scores_a, hits_a, False)
    weights_b, losses_b = softmax(scores_b, hits_b, True)
    for (low, high), first, second in zip(chunks, weights_a, weights_b):
        start, size = low * PBLK, (high - low) * PBLK
        turned[pl.ds(start, size), pl.ds(0, LANES)] = first
        rest = pl.ds(LANES, LANES // 2)
        turned[pl.ds(start, size // 2), rest] = second[:, :LANES // 2]
        turned[pl.ds(start + size // 2, size // 2), rest] = second[:, LANES // 2:]

    def slim(step):
        return remote(
            sent_slim.at[step - half], got_slim.at[step - half], e_send.at[step], e_recv.at[step],
            across(step),
        )

    def wide(step):
        return remote(
            sent_wide.at[step], got_wide.at[step], e_send.at[step], e_recv.at[step], across(step)
        )

    group = min(half, 4)

    def grads(index):
        block = turned[pl.ds(index * group * PBLK, group * PBLK), :]
        result = jnp.dot(block, q[...], preferred_element_type=jnp.float32)
        return result.reshape(group, PBLK, q.shape[1])

    def give_slim(index):
        sent_slim[pl.ds(index * group - half, group)] = grads(index).astype(jnp.bfloat16)
        for place in range(group):
            slim(index * group + place).start()

    def give_wide(index):
        sent_wide[pl.ds(index * group, group)] = grads(index)
        for place in range(group):
            step = index * group + place
            if isinstance(step, int):
                if step:
                    wide(step).start()
            else:
                pl.when(step > 0)(lambda step=step: wide(step).start())

    each(half // group, n // group, give_slim)
    each(0, half // group, give_wide)

    losses = losses_a + 0.5 * losses_b
    loss_dp[0] = jnp.broadcast_to(jnp.sum(losses, axis=1, keepdims=True), loss_dp.shape[1:])

    def loss_across(step):
        return remote(
            loss_dp.at[0], loss_dp.at[step], f_send.at[step], f_recv.at[step], across(step)
        )

    each(1, n, lambda step: loss_across(step).start())

    qgrad_ref[...] = lax.dot_general(
        turned[...], flat[...], (((0,), (0,)), ((), ())), preferred_element_type=jnp.float32
    )
    save_q = pltpu.make_async_copy(qgrad_ref, qgrad_hbm, local_sem.at[4])
    save_q.start()

    each(1, n, lambda step: passage(step).wait_send())
    for index in range(len(chunks)):
        for step in range(1, m):
            score(index, step).wait_send()
    pgrad_ref[...] = jnp.zeros_like(pgrad_ref)

    def collect(step, block):
        pick = jnp.full(block.shape, pair_ref[flip(me, step, n)], jnp.int32)
        for place in range(PB_DEV):
            pgrad_ref[pl.ds(place * PBLK, PBLK), :] += jnp.where(pick == place, block, 0.0)

    def take_wide(step):
        wide(step).wait_recv()
        collect(step, got_wide[step])

    def take_slim(step):
        slim(step).wait_recv()
        collect(step, got_slim[step - half].astype(jnp.float32))

    collect(0, sent_wide[0])
    each(1, half, take_wide)
    each(half, n, take_slim)
    save_p = pltpu.make_async_copy(pgrad_ref, pgrad_hbm, local_sem.at[5])
    save_p.start()
    each(1, n, lambda step: loss_across(step).wait_recv())
    losses = loss_dp[...]
    while losses.shape[0] > 1:
        losses = losses.reshape(losses.shape[0] // 2, 2, *losses.shape[1:])
        losses = losses[:, 0] + losses[:, 1]
    loss_ref[...] = losses[0, 0:1, 0:1] / (rows * n)
    save_loss = pltpu.make_async_copy(loss_ref, loss_hbm, local_sem.at[6])
    save_loss.start()

    each(1, n, lambda step: loss_across(step).wait_send())
    each(1, half, lambda step: wide(step).wait_send())
    each(half, n, lambda step: slim(step).wait_send())
    save_q.wait()
    save_p.wait()
    save_loss.wait()


def hand_over(loss_in, qgrad_in, pgrad_in, loss_out, qgrad_out, pgrad_out, loss, qgrad, pgrad, sems):
    parts = [(loss_in, loss, loss_out)]
    piece = 64
    for source, held, target in ((qgrad_in, qgrad, qgrad_out), (pgrad_in, pgrad, pgrad_out)):
        for start in range(0, held.shape[0], piece):
            place = pl.ds(start, piece)
            parts.append((source.at[place], held.at[place], target.at[place]))
    loads, stores = [], []
    for index, (source, held, target) in enumerate(parts):
        loads.append(pltpu.make_async_copy(source, held, sems.at[0, index]))
        stores.append(pltpu.make_async_copy(held, target, sems.at[1, index]))
    for load in loads:
        load.start()
    for load, store in zip(loads, stores):
        load.wait()
        store.start()
    for store in stores:
        store.wait()


def per_device(n, m, queries, passages, pair_block, positives):
    rows, width = queries.shape
    half, cands = n // 2, n * PBLK
    vmem, sems = pltpu.VMEM, pltpu.SemaphoreType.DMA
    bf16, f32 = jnp.bfloat16, jnp.float32
    results = [
        jax.ShapeDtypeStruct((1, 1), f32),
        jax.ShapeDtypeStruct((rows, width), f32),
        jax.ShapeDtypeStruct(passages.shape, f32),
    ]
    held = [vmem((1, 1), f32), vmem((rows, width), f32), vmem(passages.shape, f32)]
    scratch = held + [
        pltpu.SMEM((n,), jnp.int32),
        vmem((1, rows), jnp.int32),
        vmem((rows, width), bf16),
        vmem((PB_DEV, PBLK, width), bf16),
        vmem((n, PBLK, width), bf16),
        vmem((cands, width), bf16),
        vmem((cands * 3 // 2, LANES), f32),
        vmem((m, cands * 3 // 2, LANES), f32),
        vmem((cands, rows), bf16),
        vmem((half, PBLK, width), f32),
        vmem((half, PBLK, width), bf16),
        vmem((half, PBLK, width), f32),
        vmem((half, PBLK, width), bf16),
        vmem((n, 8, 128), f32),
        sems((7,)),
        sems((n,)), sems((n,)), sems((3, m)), sems((3, m)),
        sems((n,)), sems((n,)), sems((n,)), sems((n,)),
    ]
    anywhere = pl.BlockSpec(memory_space=pl.ANY)
    found = pl.pallas_call(
        functools.partial(kernel, n, m),
        out_shape=results,
        in_specs=[anywhere] * 4,
        out_specs=[anywhere] * 3,
        scratch_shapes=scratch,
        compiler_params=pltpu.CompilerParams(
            collective_id=0, has_side_effects=True,
            vmem_limit_bytes=60 << 20,
        ),
    )(queries, passages.reshape(PB_DEV, PBLK, width), pair_block.reshape(n),
      positives.reshape(1, rows))
    loss, query_grad, passage_grad = pl.pallas_call(
        hand_over,
        out_shape=results,
        in_specs=[anywhere] * 3,
        out_specs=[anywhere] * 3,
        scratch_shapes=held + [sems((2, 1 + (rows + passages.shape[0]) // 64))],
        compiler_params=pltpu.CompilerParams(vmem_limit_bytes=60 << 20),
    )(*found)
    return loss.reshape(()), query_grad, passage_grad


def solution(mesh):
    n, m = mesh.shape["dp"], mesh.shape["mp"]
    in_specs = (P("dp", "mp"), P("dp", "mp"), P(None, "dp"), P("dp"))
    out_specs = (P(), P("dp", "mp"), P("dp", "mp"))
    return jax.shard_map(
        functools.partial(per_device, n, m),
        mesh=mesh, in_specs=in_specs, out_specs=out_specs, check_vma=False,
    )
```

```python
import functools
import jax
import jax.numpy as jnp
from jax import lax
from jax.experimental import pallas as pl
from jax.experimental.pallas import tpu as pltpu
from jax.sharding import PartitionSpec as P

PBLK = 16
PB_DEV = 4
MESH = pl.DeviceIdType.MESH
UNROLL = 8
LANES = 128


def flip(index, step, count):
    result, bit = 0, 1
    while bit < count:
        mine, other = (index // bit) % 2, (step // bit) % 2
        result = result + bit * (mine + other - 2 * mine * other)
        bit *= 2
    return result


def wide_slots(count):
    return count // 2 - count // 8


def each(low, high, body):
    if high - low <= UNROLL:
        for step in range(low, high):
            body(step)
    else:
        lax.fori_loop(low, high, lambda step, carry: (body(step), carry)[1], 0)


def kernel(
    n, m, q_hbm, p_hbm, pair_hbm, pos_hbm, loss_hbm, qgrad_hbm, pgrad_hbm,
    loss_ref, qgrad_ref, pgrad_ref, pair_ref, pos_ref, q, p, outgoing, flat, part, shares, turned,
    sent_wide, sent_slim, got_wide, got_slim, loss_dp,
    local_sem, a_send, a_recv, b_send, b_recv, e_send, e_recv, f_send, f_recv,
):
    half = n // 2
    rows = q.shape[0]
    me = lax.axis_index("dp")
    mine = lax.axis_index("mp")

    def remote(src, dst, send, recv, device):
        return pltpu.make_async_remote_copy(
            src_ref=src, dst_ref=dst, send_sem=send, recv_sem=recv,
            device_id=device, device_id_type=MESH,
        )

    def across(step):
        return (flip(me, step, n), mine)

    def beside(step):
        return (me, flip(mine, step, m))

    load_p = pltpu.make_async_copy(p_hbm, p, local_sem.at[0])
    load_q = pltpu.make_async_copy(q_hbm, q, local_sem.at[1])
    load_pair = pltpu.make_async_copy(pair_hbm, pair_ref, local_sem.at[2])
    load_pos = pltpu.make_async_copy(pos_hbm, pos_ref, local_sem.at[3])
    load_pair.start()
    load_p.start()
    load_pos.start()
    load_q.start()
    barrier = pltpu.get_barrier_semaphore()

    def greet(step):
        pl.semaphore_signal(barrier, inc=1, device_id=across(step), device_id_type=MESH)

    each(1, n, greet)
    for step in range(1, m):
        pl.semaphore_signal(barrier, inc=1, device_id=beside(step), device_id_type=MESH)

    def slot(step):
        return pl.ds(step * PBLK, PBLK)

    def chosen(step):
        return p[pair_ref[flip(me, step, n)]]

    load_pair.wait()
    load_p.wait()

    def pack(step):
        outgoing[step] = chosen(step)

    each(1, n, pack)
    flat[0:PBLK, :] = chosen(0)
    pl.semaphore_wait(barrier, n - 1 + m - 1)

    def passage(step):
        return remote(
            outgoing.at[step], flat.at[slot(step)], a_send.at[step], a_recv.at[step], across(step)
        )

    passage(half).start()
    each(1, half, lambda step: passage(step).start())
    each(half + 1, n, lambda step: passage(step).start())

    load_pos.wait()
    load_q.wait()

    ends = (0, half, half + n // 4, n - n // 8, n)
    chunks = tuple(zip(ends[:-1], ends[1:]))

    def packed(index):
        low, high = chunks[index]
        size = (high - low) * PBLK
        return pl.ds(low * PBLK * 3 // 2, size * 3 // 2), size

    def score(index, step):
        place, _ = packed(index)
        return remote(
            part.at[place], shares.at[step, place], b_send.at[index, step],
            b_recv.at[index, step], beside(step),
        )

    for index, (low, high) in enumerate(chunks):
        each(max(low, 1), high, lambda step: passage(step).wait_recv())
        block = lax.dot_general(
            flat[low * PBLK:high * PBLK, :], q[...], (((1,), (1,)), ((), ())),
            preferred_element_type=jnp.float32,
        )
        place, size = packed(index)
        part[pl.ds(place.start, size), :] = block[:, :LANES]
        part[pl.ds(place.start + size, size // 2), :] = jnp.concatenate(
            [block[:size // 2, LANES:], block[size // 2:, LANES:]], axis=1
        )
        for step in reversed(range(1, m)):
            score(index, step).start()

    def swap(row):
        return jnp.concatenate([row[:, LANES // 2:], row[:, :LANES // 2]], axis=1)

    spots = pos_ref[...] ^ (me * PBLK)
    spots_a = spots[:, :LANES]
    spots_b = jnp.concatenate([spots[:, LANES:], spots[:, LANES:]], axis=1)
    scores_a, scores_b, hits_a, hits_b = [], [], [], []
    for index, (low, high) in enumerate(chunks):
        place, size = packed(index)
        for step in range(1, m):
            score(index, step).wait_recv()
        terms = [part[place, :]] + [shares[step, place, :] for step in range(1, m)]
        while len(terms) > 1:
            terms = [first + second for first, second in zip(terms[::2], terms[1::2])]
        scores_a.append(terms[0][:size])
        scores_b.append(terms[0][size:])
        down = lax.broadcasted_iota(jnp.int32, (size, LANES), 0) + low * PBLK
        hits_a.append(down == spots_a)
        down = lax.broadcasted_iota(jnp.int32, (size // 2, LANES), 0) + low * PBLK
        right = lax.broadcasted_iota(jnp.int32, (size // 2, LANES), 1) // (LANES // 2)
        hits_b.append(down + right * (size // 2) == spots_b)

    def gathered(blocks, combine, reduce):
        return functools.reduce(combine, [reduce(block, axis=0, keepdims=True) for block in blocks])

    def softmax(scores, hits, paired):
        top = gathered(scores, jnp.maximum, jnp.max)
        if paired:
            top = jnp.maximum(top, swap(top))
        raised = [jnp.exp(block - top) for block in scores]
        total = gathered(raised, jnp.add, jnp.sum)
        picked = [jnp.where(hit, block, 0.0) for hit, block in zip(hits, scores)]
        positive = gathered(picked, jnp.add, jnp.sum)
        if paired:
            total = total + swap(total)
            positive = positive + swap(positive)
        inverse = 1.0 / total
        weights = [
            (block * inverse - hit.astype(jnp.float32)).astype(jnp.bfloat16)
            for block, hit in zip(raised, hits)
        ]
        return weights, top + jnp.log(total) - positive

    weights_a, losses_a = softmax(scores_a, hits_a, False)
    weights_b, losses_b = softmax(scores_b, hits_b, True)
    for (low, high), first, second in zip(chunks, weights_a, weights_b):
        start, size = low * PBLK, (high - low) * PBLK
        turned[pl.ds(start, size), pl.ds(0, LANES)] = first
        rest = pl.ds(LANES, LANES // 2)
        turned[pl.ds(start, size // 2), rest] = second[:, :LANES // 2]
        turned[pl.ds(start + size // 2, size // 2), rest] = second[:, LANES // 2:]

    wide = wide_slots(n)

    def gradient(step, slim):
        if slim:
            source, target = sent_slim.at[step - wide], got_slim.at[step - wide]
        else:
            source, target = sent_wide.at[step], got_wide.at[step]
        return remote(source, target, e_send.at[step], e_recv.at[step], across(step))

    group = min(half, 4)

    def give(index, slim):
        block = turned[pl.ds(index * group * PBLK, group * PBLK), :]
        result = jnp.dot(block, q[...], preferred_element_type=jnp.float32)
        result = result.reshape(group, PBLK, q.shape[1])
        for place in range(group):
            step = index * group + place
            fixed = isinstance(step, int)
            narrow = step >= wide if fixed else slim
            if narrow:
                sent_slim[step - wide] = result[place].astype(jnp.bfloat16)
            else:
                sent_wide[step] = result[place]
            if not fixed:
                pl.when(step > 0)(lambda step=step: gradient(step, narrow).start())
            elif step:
                gradient(step, narrow).start()

    wide_groups = -(-wide // group)
    each(half // group, n // group, lambda index: give(index, True))
    each(wide_groups, half // group, lambda index: give(index, True))
    each(0, wide_groups, lambda index: give(index, False))

    losses = losses_a + 0.5 * losses_b
    loss_dp[0] = jnp.broadcast_to(jnp.sum(losses, axis=1, keepdims=True), loss_dp.shape[1:])

    def loss_across(step):
        return remote(
            loss_dp.at[0], loss_dp.at[step], f_send.at[step], f_recv.at[step], across(step)
        )

    each(1, n, lambda step: loss_across(step).start())

    qgrad_ref[...] = lax.dot_general(
        turned[...], flat[...], (((0,), (0,)), ((), ())), preferred_element_type=jnp.float32
    )
    save_q = pltpu.make_async_copy(qgrad_ref, qgrad_hbm, local_sem.at[4])
    save_q.start()

    each(1, n, lambda step: passage(step).wait_send())
    for index in range(len(chunks)):
        for step in range(1, m):
            score(index, step).wait_send()
    pgrad_ref[...] = jnp.zeros_like(pgrad_ref)

    def collect(step, block):
        pick = jnp.full(block.shape, pair_ref[flip(me, step, n)], jnp.int32)
        for place in range(PB_DEV):
            pgrad_ref[pl.ds(place * PBLK, PBLK), :] += jnp.where(pick == place, block, 0.0)

    def take_wide(step):
        gradient(step, False).wait_recv()
        collect(step, got_wide[step])

    def take_slim(step):
        gradient(step, True).wait_recv()
        collect(step, got_slim[step - wide].astype(jnp.float32))

    collect(0, sent_wide[0])
    each(1, wide, take_wide)
    each(wide, n, take_slim)
    save_p = pltpu.make_async_copy(pgrad_ref, pgrad_hbm, local_sem.at[5])
    save_p.start()
    each(1, n, lambda step: loss_across(step).wait_recv())
    losses = loss_dp[...]
    while losses.shape[0] > 1:
        losses = losses.reshape(losses.shape[0] // 2, 2, *losses.shape[1:])
        losses = losses[:, 0] + losses[:, 1]
    loss_ref[...] = losses[0, 0:1, 0:1] / (rows * n)
    save_loss = pltpu.make_async_copy(loss_ref, loss_hbm, local_sem.at[6])
    save_loss.start()

    each(1, n, lambda step: loss_across(step).wait_send())
    each(1, wide, lambda step: gradient(step, False).wait_send())
    each(wide, n, lambda step: gradient(step, True).wait_send())
    save_q.wait()
    save_p.wait()
    save_loss.wait()


def hand_over(loss_in, qgrad_in, pgrad_in, loss_out, qgrad_out, pgrad_out, loss, qgrad, pgrad, sems):
    parts = []
    for source, held, target in ((qgrad_in, qgrad, qgrad_out), (pgrad_in, pgrad, pgrad_out)):
        piece = held.shape[0] // 2
        for start in range(0, held.shape[0], piece):
            place = pl.ds(start, piece)
            parts.append((source.at[place], held.at[place], target.at[place]))
    parts.append((loss_in, loss, loss_out))
    loads, stores = [], []
    for index, (source, held, target) in enumerate(parts):
        loads.append(pltpu.make_async_copy(source, held, sems.at[0, index]))
        stores.append(pltpu.make_async_copy(held, target, sems.at[1, index]))
    for load in loads:
        load.start()
    for load, store in zip(loads, stores):
        load.wait()
        store.start()
    for store in stores:
        store.wait()


def per_device(n, m, queries, passages, pair_block, positives):
    rows, width = queries.shape
    wide, cands = wide_slots(n), n * PBLK
    vmem, sems = pltpu.VMEM, pltpu.SemaphoreType.DMA
    bf16, f32 = jnp.bfloat16, jnp.float32
    results = [
        jax.ShapeDtypeStruct((1, 1), f32),
        jax.ShapeDtypeStruct((rows, width), f32),
        jax.ShapeDtypeStruct(passages.shape, f32),
    ]
    held = [vmem((1, 1), f32), vmem((rows, width), f32), vmem(passages.shape, f32)]
    scratch = held + [
        pltpu.SMEM((n,), jnp.int32),
        vmem((1, rows), jnp.int32),
        vmem((rows, width), bf16),
        vmem((PB_DEV, PBLK, width), bf16),
        vmem((n, PBLK, width), bf16),
        vmem((cands, width), bf16),
        vmem((cands * 3 // 2, LANES), f32),
        vmem((m, cands * 3 // 2, LANES), f32),
        vmem((cands, rows), bf16),
        vmem((wide, PBLK, width), f32),
        vmem((n - wide, PBLK, width), bf16),
        vmem((wide, PBLK, width), f32),
        vmem((n - wide, PBLK, width), bf16),
        vmem((n, 8, 128), f32),
        sems((7,)),
        sems((n,)), sems((n,)), sems((4, m)), sems((4, m)),
        sems((n,)), sems((n,)), sems((n,)), sems((n,)),
    ]
    anywhere = pl.BlockSpec(memory_space=pl.ANY)
    found = pl.pallas_call(
        functools.partial(kernel, n, m),
        out_shape=results,
        in_specs=[anywhere] * 4,
        out_specs=[anywhere] * 3,
        scratch_shapes=scratch,
        compiler_params=pltpu.CompilerParams(
            collective_id=0, has_side_effects=True,
            vmem_limit_bytes=60 << 20,
        ),
    )(queries, passages.reshape(PB_DEV, PBLK, width), pair_block.reshape(n),
      positives.reshape(1, rows))
    loss, query_grad, passage_grad = pl.pallas_call(
        hand_over,
        out_shape=results,
        in_specs=[anywhere] * 3,
        out_specs=[anywhere] * 3,
        scratch_shapes=held + [sems((2, 5))],
        compiler_params=pltpu.CompilerParams(vmem_limit_bytes=60 << 20),
    )(*found)
    return loss.reshape(()), query_grad, passage_grad


def solution(mesh):
    n, m = mesh.shape["dp"], mesh.shape["mp"]
    in_specs = (P("dp", "mp"), P("dp", "mp"), P(None, "dp"), P("dp"))
    out_specs = (P(), P("dp", "mp"), P("dp", "mp"))
    return jax.shard_map(
        functools.partial(per_device, n, m),
        mesh=mesh, in_specs=in_specs, out_specs=out_specs, check_vma=False,
    )
```

```python
import functools
import jax
import jax.numpy as jnp
from jax import lax
from jax.experimental import pallas as pl
from jax.experimental.pallas import tpu as pltpu
from jax.sharding import PartitionSpec as P

PBLK = 16
PB_DEV = 4
MESH = pl.DeviceIdType.MESH
UNROLL = 8
LANES = 128


def flip(index, step, count):
    result, bit = 0, 1
    while bit < count:
        mine, other = (index // bit) % 2, (step // bit) % 2
        result = result + bit * (mine + other - 2 * mine * other)
        bit *= 2
    return result


def wide_slots(count):
    return count // 2 - count // 8


def each(low, high, body):
    if high - low <= UNROLL:
        for step in range(low, high):
            body(step)
    else:
        lax.fori_loop(low, high, lambda step, carry: (body(step), carry)[1], 0)


def kernel(
    n, m, q_hbm, p_hbm, pair_hbm, pos_hbm, loss_ref, qgrad_ref, pgrad_ref, pair_ref, pos_ref, q, p, outgoing, flat, part, shares, turned,
    sent_wide, sent_slim, got_wide, got_slim, loss_dp,
    local_sem, a_send, a_recv, b_send, b_recv, e_send, e_recv, f_send, f_recv,
):
    half = n // 2
    rows = q.shape[0]
    me = lax.axis_index("dp")
    mine = lax.axis_index("mp")

    def remote(src, dst, send, recv, device):
        return pltpu.make_async_remote_copy(
            src_ref=src, dst_ref=dst, send_sem=send, recv_sem=recv,
            device_id=device, device_id_type=MESH,
        )

    def across(step):
        return (flip(me, step, n), mine)

    def beside(step):
        return (me, flip(mine, step, m))

    load_p = pltpu.make_async_copy(p_hbm, p, local_sem.at[0])
    load_q = pltpu.make_async_copy(q_hbm, q, local_sem.at[1])
    load_pair = pltpu.make_async_copy(pair_hbm, pair_ref, local_sem.at[2])
    load_pos = pltpu.make_async_copy(pos_hbm, pos_ref, local_sem.at[3])
    load_pair.start()
    load_p.start()
    load_pos.start()
    load_q.start()
    barrier = pltpu.get_barrier_semaphore()

    def greet(step):
        pl.semaphore_signal(barrier, inc=1, device_id=across(step), device_id_type=MESH)

    each(1, n, greet)
    for step in range(1, m):
        pl.semaphore_signal(barrier, inc=1, device_id=beside(step), device_id_type=MESH)

    def slot(step):
        return pl.ds(step * PBLK, PBLK)

    def chosen(step):
        return p[pair_ref[flip(me, step, n)]]

    load_pair.wait()
    load_p.wait()

    def pack(step):
        outgoing[step] = chosen(step)

    each(1, n, pack)
    flat[0:PBLK, :] = chosen(0)
    pl.semaphore_wait(barrier, n - 1 + m - 1)

    def passage(step):
        return remote(
            outgoing.at[step], flat.at[slot(step)], a_send.at[step], a_recv.at[step], across(step)
        )

    passage(half).start()
    each(1, half, lambda step: passage(step).start())
    each(half + 1, n, lambda step: passage(step).start())

    load_pos.wait()
    load_q.wait()

    ends = (0, half, half + n // 4, n - n // 8, n)
    chunks = tuple(zip(ends[:-1], ends[1:]))

    def packed(index):
        low, high = chunks[index]
        size = (high - low) * PBLK
        return pl.ds(low * PBLK * 3 // 2, size * 3 // 2), size

    def score(index, step):
        place, _ = packed(index)
        return remote(
            part.at[place], shares.at[step, place], b_send.at[index, step],
            b_recv.at[index, step], beside(step),
        )

    for index, (low, high) in enumerate(chunks):
        each(max(low, 1), high, lambda step: passage(step).wait_recv())
        block = lax.dot_general(
            flat[low * PBLK:high * PBLK, :], q[...], (((1,), (1,)), ((), ())),
            preferred_element_type=jnp.float32,
        )
        place, size = packed(index)
        part[pl.ds(place.start, size), :] = block[:, :LANES]
        part[pl.ds(place.start + size, size // 2), :] = jnp.concatenate(
            [block[:size // 2, LANES:], block[size // 2:, LANES:]], axis=1
        )
        for step in reversed(range(1, m)):
            score(index, step).start()

    def swap(row):
        return jnp.concatenate([row[:, LANES // 2:], row[:, :LANES // 2]], axis=1)

    spots = pos_ref[...] ^ (me * PBLK)
    spots_a = spots[:, :LANES]
    spots_b = jnp.concatenate([spots[:, LANES:], spots[:, LANES:]], axis=1)
    scores_a, scores_b, hits_a, hits_b = [], [], [], []
    for index, (low, high) in enumerate(chunks):
        place, size = packed(index)
        for step in range(1, m):
            score(index, step).wait_recv()
        terms = [part[place, :]] + [shares[step, place, :] for step in range(1, m)]
        while len(terms) > 1:
            terms = [first + second for first, second in zip(terms[::2], terms[1::2])]
        scores_a.append(terms[0][:size])
        scores_b.append(terms[0][size:])
        down = lax.broadcasted_iota(jnp.int32, (size, LANES), 0) + low * PBLK
        hits_a.append(down == spots_a)
        down = lax.broadcasted_iota(jnp.int32, (size // 2, LANES), 0) + low * PBLK
        right = lax.broadcasted_iota(jnp.int32, (size // 2, LANES), 1) // (LANES // 2)
        hits_b.append(down + right * (size // 2) == spots_b)

    def gathered(blocks, combine, reduce):
        return functools.reduce(combine, [reduce(block, axis=0, keepdims=True) for block in blocks])

    def softmax(scores, hits, paired):
        top = gathered(scores, jnp.maximum, jnp.max)
        if paired:
            top = jnp.maximum(top, swap(top))
        raised = [jnp.exp(block - top) for block in scores]
        total = gathered(raised, jnp.add, jnp.sum)
        picked = [jnp.where(hit, block, 0.0) for hit, block in zip(hits, scores)]
        positive = gathered(picked, jnp.add, jnp.sum)
        if paired:
            total = total + swap(total)
            positive = positive + swap(positive)
        inverse = 1.0 / total
        weights = [
            (block * inverse - hit.astype(jnp.float32)).astype(jnp.bfloat16)
            for block, hit in zip(raised, hits)
        ]
        return weights, top + jnp.log(total) - positive

    weights_a, losses_a = softmax(scores_a, hits_a, False)
    weights_b, losses_b = softmax(scores_b, hits_b, True)
    for (low, high), first, second in zip(chunks, weights_a, weights_b):
        start, size = low * PBLK, (high - low) * PBLK
        turned[pl.ds(start, size), pl.ds(0, LANES)] = first
        rest = pl.ds(LANES, LANES // 2)
        turned[pl.ds(start, size // 2), rest] = second[:, :LANES // 2]
        turned[pl.ds(start + size // 2, size // 2), rest] = second[:, LANES // 2:]

    wide = wide_slots(n)

    def gradient(step, slim):
        if slim:
            source, target = sent_slim.at[step - wide], got_slim.at[step - wide]
        else:
            source, target = sent_wide.at[step], got_wide.at[step]
        return remote(source, target, e_send.at[step], e_recv.at[step], across(step))

    group = min(half, 4)

    def give(index, slim):
        block = turned[pl.ds(index * group * PBLK, group * PBLK), :]
        result = jnp.dot(block, q[...], preferred_element_type=jnp.float32)
        result = result.reshape(group, PBLK, q.shape[1])
        for place in range(group):
            step = index * group + place
            fixed = isinstance(step, int)
            narrow = step >= wide if fixed else slim
            if narrow:
                sent_slim[step - wide] = result[place].astype(jnp.bfloat16)
            else:
                sent_wide[step] = result[place]
            if not fixed:
                pl.when(step > 0)(lambda step=step: gradient(step, narrow).start())
            elif step:
                gradient(step, narrow).start()

    wide_groups = -(-wide // group)
    each(half // group, n // group, lambda index: give(index, True))
    each(wide_groups, half // group, lambda index: give(index, True))
    each(0, wide_groups, lambda index: give(index, False))

    losses = losses_a + 0.5 * losses_b
    loss_dp[0] = jnp.broadcast_to(jnp.sum(losses, axis=1, keepdims=True), loss_dp.shape[1:])

    def loss_across(step):
        return remote(
            loss_dp.at[0], loss_dp.at[step], f_send.at[step], f_recv.at[step], across(step)
        )

    each(1, n, lambda step: loss_across(step).start())

    qgrad_ref[...] = lax.dot_general(
        turned[...], flat[...], (((0,), (0,)), ((), ())), preferred_element_type=jnp.float32
    )

    each(1, n, lambda step: passage(step).wait_send())
    for index in range(len(chunks)):
        for step in range(1, m):
            score(index, step).wait_send()
    pgrad_ref[...] = jnp.zeros_like(pgrad_ref)

    def collect(step, block):
        pick = jnp.full(block.shape, pair_ref[flip(me, step, n)], jnp.int32)
        for place in range(PB_DEV):
            pgrad_ref[pl.ds(place * PBLK, PBLK), :] += jnp.where(pick == place, block, 0.0)

    def take_wide(step):
        gradient(step, False).wait_recv()
        collect(step, got_wide[step])

    def take_slim(step):
        gradient(step, True).wait_recv()
        collect(step, got_slim[step - wide].astype(jnp.float32))

    collect(0, sent_wide[0])
    each(1, wide, take_wide)
    each(wide, n, take_slim)
    each(1, n, lambda step: loss_across(step).wait_recv())
    losses = loss_dp[...]
    while losses.shape[0] > 1:
        losses = losses.reshape(losses.shape[0] // 2, 2, *losses.shape[1:])
        losses = losses[:, 0] + losses[:, 1]
    loss_ref[...] = losses[0] / (rows * n)

    each(1, n, lambda step: loss_across(step).wait_send())
    each(1, wide, lambda step: gradient(step, False).wait_send())
    each(wide, n, lambda step: gradient(step, True).wait_send())


def hand_over(loss_in, qgrad_in, pgrad_in, loss_out, qgrad_out, pgrad_out, loss, sems):
    loss[...] = loss_in[0:1, 0:1]
    pairs = ((qgrad_in, qgrad_out), (pgrad_in, pgrad_out), (loss, loss_out))
    copies = [
        pltpu.make_async_copy(source, target, sems.at[index])
        for index, (source, target) in enumerate(pairs)
    ]
    for copy in copies:
        copy.start()
    for copy in copies:
        copy.wait()


def per_device(n, m, queries, passages, pair_block, positives):
    rows, width = queries.shape
    wide, cands = wide_slots(n), n * PBLK
    vmem, sems = pltpu.VMEM, pltpu.SemaphoreType.DMA
    bf16, f32 = jnp.bfloat16, jnp.float32
    results = [
        jax.ShapeDtypeStruct((1, 1), f32),
        jax.ShapeDtypeStruct((rows, width), f32),
        jax.ShapeDtypeStruct(passages.shape, f32),
    ]
    held = [vmem((8, 128), f32), vmem((rows, width), f32), vmem(passages.shape, f32)]
    scratch = [
        pltpu.SMEM((n,), jnp.int32),
        vmem((1, rows), jnp.int32),
        vmem((rows, width), bf16),
        vmem((PB_DEV, PBLK, width), bf16),
        vmem((n, PBLK, width), bf16),
        vmem((cands, width), bf16),
        vmem((cands * 3 // 2, LANES), f32),
        vmem((m, cands * 3 // 2, LANES), f32),
        vmem((cands, rows), bf16),
        vmem((wide, PBLK, width), f32),
        vmem((n - wide, PBLK, width), bf16),
        vmem((wide, PBLK, width), f32),
        vmem((n - wide, PBLK, width), bf16),
        vmem((n, 8, 128), f32),
        sems((4,)),
        sems((n,)), sems((n,)), sems((4, m)), sems((4, m)),
        sems((n,)), sems((n,)), sems((n,)), sems((n,)),
    ]
    anywhere = pl.BlockSpec(memory_space=pl.ANY)
    inside = pl.BlockSpec(memory_space=pltpu.VMEM)
    found = pl.pallas_call(
        functools.partial(kernel, n, m),
        out_shape=held,
        in_specs=[anywhere] * 4,
        out_specs=[inside] * 3,
        scratch_shapes=scratch,
        compiler_params=pltpu.CompilerParams(
            collective_id=0, has_side_effects=True,
            vmem_limit_bytes=60 << 20,
        ),
    )(queries, passages.reshape(PB_DEV, PBLK, width), pair_block.reshape(n),
      positives.reshape(1, rows))
    loss, query_grad, passage_grad = pl.pallas_call(
        hand_over,
        out_shape=results,
        in_specs=[inside, anywhere, anywhere],
        out_specs=[anywhere] * 3,
        scratch_shapes=[vmem((1, 1), f32), sems((3,))],
        compiler_params=pltpu.CompilerParams(vmem_limit_bytes=1 << 20),
    )(*found)
    return loss.reshape(()), query_grad, passage_grad


def solution(mesh):
    n, m = mesh.shape["dp"], mesh.shape["mp"]
    in_specs = (P("dp", "mp"), P("dp", "mp"), P(None, "dp"), P("dp"))
    out_specs = (P(), P("dp", "mp"), P("dp", "mp"))
    return jax.shard_map(
        functools.partial(per_device, n, m),
        mesh=mesh, in_specs=in_specs, out_specs=out_specs, check_vma=False,
    )
```

```python
import functools
import jax
import jax.numpy as jnp
from jax import lax
from jax.experimental import pallas as pl
from jax.experimental.pallas import tpu as pltpu
from jax.sharding import PartitionSpec as P

PBLK = 16
PB_DEV = 4
MESH = pl.DeviceIdType.MESH
UNROLL = 8
LANES = 128


def flip(index, step, count):
    result, bit = 0, 1
    while bit < count:
        mine, other = (index // bit) % 2, (step // bit) % 2
        result = result + bit * (mine + other - 2 * mine * other)
        bit *= 2
    return result


def wide_slots(count):
    return count // 2 - count // 8


def each(low, high, body):
    if high - low <= UNROLL:
        for step in range(low, high):
            body(step)
    else:
        lax.fori_loop(low, high, lambda step, carry: (body(step), carry)[1], 0)


def kernel(
    n, m, q_hbm, p_hbm, pair_hbm, pos_hbm, loss_ref, qgrad_ref, pgrad_ref, pair_ref, pos_ref, q, p, outgoing, flat, part, shares, turned,
    sent_wide, sent_slim, got_wide, got_slim, loss_dp,
    local_sem, a_send, a_recv, b_send, b_recv, e_send, e_recv, f_send, f_recv,
):
    half = n // 2
    rows = q.shape[0]
    me = lax.axis_index("dp")
    mine = lax.axis_index("mp")

    def remote(src, dst, send, recv, device):
        return pltpu.make_async_remote_copy(
            src_ref=src, dst_ref=dst, send_sem=send, recv_sem=recv,
            device_id=device, device_id_type=MESH,
        )

    def across(step):
        return (flip(me, step, n), mine)

    def beside(step):
        return (me, flip(mine, step, m))

    load_p = pltpu.make_async_copy(p_hbm, p, local_sem.at[0])
    load_q = pltpu.make_async_copy(q_hbm, q, local_sem.at[1])
    load_pair = pltpu.make_async_copy(pair_hbm, pair_ref, local_sem.at[2])
    load_pos = pltpu.make_async_copy(pos_hbm, pos_ref, local_sem.at[3])
    load_pair.start()
    load_p.start()
    load_pos.start()
    load_q.start()
    barrier = pltpu.get_barrier_semaphore()

    def greet(step):
        pl.semaphore_signal(barrier, inc=1, device_id=across(step), device_id_type=MESH)

    each(1, n, greet)
    for step in range(1, m):
        pl.semaphore_signal(barrier, inc=1, device_id=beside(step), device_id_type=MESH)

    def slot(step):
        return pl.ds(step * PBLK, PBLK)

    def chosen(step):
        return p[pair_ref[flip(me, step, n)]]

    load_pair.wait()
    load_p.wait()

    def pack(step):
        outgoing[step] = chosen(step)

    each(1, n, pack)
    flat[0:PBLK, :] = chosen(0)
    pl.semaphore_wait(barrier, n - 1 + m - 1)

    def passage(step):
        return remote(
            outgoing.at[step], flat.at[slot(step)], a_send.at[step], a_recv.at[step], across(step)
        )

    passage(half).start()
    each(1, half, lambda step: passage(step).start())
    each(half + 1, n, lambda step: passage(step).start())

    load_pos.wait()
    load_q.wait()

    ends = (0, half, half + n // 4, n - n // 8, n)
    chunks = tuple(zip(ends[:-1], ends[1:]))

    def packed(index):
        low, high = chunks[index]
        size = (high - low) * PBLK
        return pl.ds(low * PBLK * 3 // 2, size * 3 // 2), size

    def score(index, step):
        place, _ = packed(index)
        return remote(
            part.at[place], shares.at[step, place], b_send.at[index, step],
            b_recv.at[index, step], beside(step),
        )

    for index, (low, high) in enumerate(chunks):
        each(max(low, 1), high, lambda step: passage(step).wait_recv())
        block = lax.dot_general(
            flat[low * PBLK:high * PBLK, :], q[...], (((1,), (1,)), ((), ())),
            preferred_element_type=jnp.float32,
        )
        place, size = packed(index)
        part[pl.ds(place.start, size), :] = block[:, :LANES]
        part[pl.ds(place.start + size, size // 2), :] = jnp.concatenate(
            [block[:size // 2, LANES:], block[size // 2:, LANES:]], axis=1
        )
        for step in reversed(range(1, m)):
            score(index, step).start()

    def swap(row):
        return jnp.concatenate([row[:, LANES // 2:], row[:, :LANES // 2]], axis=1)

    spots = pos_ref[...] ^ (me * PBLK)
    spots_a = spots[:, :LANES]
    spots_b = jnp.concatenate([spots[:, LANES:], spots[:, LANES:]], axis=1)
    scores_a, scores_b, hits_a, hits_b = [], [], [], []
    for index, (low, high) in enumerate(chunks):
        place, size = packed(index)
        for step in range(1, m):
            score(index, step).wait_recv()
        terms = [part[place, :]] + [shares[step, place, :] for step in range(1, m)]
        while len(terms) > 1:
            terms = [first + second for first, second in zip(terms[::2], terms[1::2])]
        scores_a.append(terms[0][:size])
        scores_b.append(terms[0][size:])
        down = lax.broadcasted_iota(jnp.int32, (size, LANES), 0) + low * PBLK
        hits_a.append(down == spots_a)
        down = lax.broadcasted_iota(jnp.int32, (size // 2, LANES), 0) + low * PBLK
        right = lax.broadcasted_iota(jnp.int32, (size // 2, LANES), 1) // (LANES // 2)
        hits_b.append(down + right * (size // 2) == spots_b)

    def gathered(blocks, combine, reduce):
        return functools.reduce(combine, [reduce(block, axis=0, keepdims=True) for block in blocks])

    def softmax(scores, hits, paired):
        top = gathered(scores, jnp.maximum, jnp.max)
        if paired:
            top = jnp.maximum(top, swap(top))
        raised = [jnp.exp(block - top) for block in scores]
        total = gathered(raised, jnp.add, jnp.sum)
        picked = [jnp.where(hit, block, 0.0) for hit, block in zip(hits, scores)]
        positive = gathered(picked, jnp.add, jnp.sum)
        if paired:
            total = total + swap(total)
            positive = positive + swap(positive)
        inverse = 1.0 / total
        weights = [
            (block * inverse - hit.astype(jnp.float32)).astype(jnp.bfloat16)
            for block, hit in zip(raised, hits)
        ]
        return weights, top + jnp.log(total) - positive

    weights_a, losses_a = softmax(scores_a, hits_a, False)
    weights_b, losses_b = softmax(scores_b, hits_b, True)
    for (low, high), first, second in zip(chunks, weights_a, weights_b):
        start, size = low * PBLK, (high - low) * PBLK
        turned[pl.ds(start, size), pl.ds(0, LANES)] = first
        rest = pl.ds(LANES, LANES // 2)
        turned[pl.ds(start, size // 2), rest] = second[:, :LANES // 2]
        turned[pl.ds(start + size // 2, size // 2), rest] = second[:, LANES // 2:]

    wide = wide_slots(n)

    def gradient(step, slim):
        if slim:
            source, target = sent_slim.at[step - wide], got_slim.at[step - wide]
        else:
            source, target = sent_wide.at[step], got_wide.at[step]
        return remote(source, target, e_send.at[step], e_recv.at[step], across(step))

    group = min(half, 4)

    def give(index, slim):
        block = turned[pl.ds(index * group * PBLK, group * PBLK), :]
        result = jnp.dot(block, q[...], preferred_element_type=jnp.float32)
        result = result.reshape(group, PBLK, q.shape[1])
        for place in range(group):
            step = index * group + place
            fixed = isinstance(step, int)
            narrow = step >= wide if fixed else slim
            if narrow:
                sent_slim[step - wide] = result[place].astype(jnp.bfloat16)
            else:
                sent_wide[step] = result[place]
            if not fixed:
                pl.when(step > 0)(lambda step=step: gradient(step, narrow).start())

    def begin(*steps):
        for step in steps:
            gradient(step, step >= wide).start()

    wide_groups = -(-wide // group)
    if n <= UNROLL:
        order = [step for near in range(half) for step in (near, half + near)][1:]
        early = [half, half + 1]
        for index in range(half // group, n // group):
            give(index, True)
        begin(*early)
        for index in range(half // group):
            give(index, False)
        begin(*[step for step in order if step not in early])
    else:
        lax.fori_loop(half // group, n // group, lambda index, carry: (give(index, True), carry)[1], 0)
        lax.fori_loop(wide_groups, half // group, lambda index, carry: (give(index, True), carry)[1], 0)
        lax.fori_loop(0, wide_groups, lambda index, carry: (give(index, False), carry)[1], 0)

    losses = losses_a + 0.5 * losses_b
    loss_dp[0] = jnp.broadcast_to(jnp.sum(losses, axis=1, keepdims=True), loss_dp.shape[1:])

    def loss_across(step):
        return remote(
            loss_dp.at[0], loss_dp.at[step], f_send.at[step], f_recv.at[step], across(step)
        )

    each(1, n, lambda step: loss_across(step).start())

    qgrad_ref[...] = lax.dot_general(
        turned[...], flat[...], (((0,), (0,)), ((), ())), preferred_element_type=jnp.float32
    )

    each(1, n, lambda step: passage(step).wait_send())
    for index in range(len(chunks)):
        for step in range(1, m):
            score(index, step).wait_send()
    pgrad_ref[...] = jnp.zeros_like(pgrad_ref)

    def collect(step, block):
        pick = jnp.full(block.shape, pair_ref[flip(me, step, n)], jnp.int32)
        for place in range(PB_DEV):
            pgrad_ref[pl.ds(place * PBLK, PBLK), :] += jnp.where(pick == place, block, 0.0)

    def take_wide(step):
        gradient(step, False).wait_recv()
        collect(step, got_wide[step])

    def take_slim(step):
        gradient(step, True).wait_recv()
        collect(step, got_slim[step - wide].astype(jnp.float32))

    collect(0, sent_wide[0])
    each(1, wide, take_wide)
    each(wide, n, take_slim)
    each(1, n, lambda step: loss_across(step).wait_recv())
    losses = loss_dp[...]
    while losses.shape[0] > 1:
        losses = losses.reshape(losses.shape[0] // 2, 2, *losses.shape[1:])
        losses = losses[:, 0] + losses[:, 1]
    loss_ref[...] = losses[0] / (rows * n)

    each(1, n, lambda step: loss_across(step).wait_send())
    each(1, wide, lambda step: gradient(step, False).wait_send())
    each(wide, n, lambda step: gradient(step, True).wait_send())


def hand_over(loss_in, qgrad_in, pgrad_in, loss_out, qgrad_out, pgrad_out, loss, sems):
    loss[...] = loss_in[0:1, 0:1]
    pairs = ((qgrad_in, qgrad_out), (pgrad_in, pgrad_out), (loss, loss_out))
    copies = [
        pltpu.make_async_copy(source, target, sems.at[index])
        for index, (source, target) in enumerate(pairs)
    ]
    for copy in copies:
        copy.start()
    for copy in copies:
        copy.wait()


def per_device(n, m, queries, passages, pair_block, positives):
    rows, width = queries.shape
    wide, cands = wide_slots(n), n * PBLK
    vmem, sems = pltpu.VMEM, pltpu.SemaphoreType.DMA
    bf16, f32 = jnp.bfloat16, jnp.float32
    results = [
        jax.ShapeDtypeStruct((1, 1), f32),
        jax.ShapeDtypeStruct((rows, width), f32),
        jax.ShapeDtypeStruct(passages.shape, f32),
    ]
    held = [vmem((8, 128), f32), vmem((rows, width), f32), vmem(passages.shape, f32)]
    scratch = [
        pltpu.SMEM((n,), jnp.int32),
        vmem((1, rows), jnp.int32),
        vmem((rows, width), bf16),
        vmem((PB_DEV, PBLK, width), bf16),
        vmem((n, PBLK, width), bf16),
        vmem((cands, width), bf16),
        vmem((cands * 3 // 2, LANES), f32),
        vmem((m, cands * 3 // 2, LANES), f32),
        vmem((cands, rows), bf16),
        vmem((wide, PBLK, width), f32),
        vmem((n - wide, PBLK, width), bf16),
        vmem((wide, PBLK, width), f32),
        vmem((n - wide, PBLK, width), bf16),
        vmem((n, 8, 128), f32),
        sems((4,)),
        sems((n,)), sems((n,)), sems((4, m)), sems((4, m)),
        sems((n,)), sems((n,)), sems((n,)), sems((n,)),
    ]
    anywhere = pl.BlockSpec(memory_space=pl.ANY)
    inside = pl.BlockSpec(memory_space=pltpu.VMEM)
    found = pl.pallas_call(
        functools.partial(kernel, n, m),
        out_shape=held,
        in_specs=[anywhere] * 4,
        out_specs=[inside] * 3,
        scratch_shapes=scratch,
        compiler_params=pltpu.CompilerParams(
            collective_id=0, has_side_effects=True,
            vmem_limit_bytes=60 << 20,
        ),
    )(queries, passages.reshape(PB_DEV, PBLK, width), pair_block.reshape(n),
      positives.reshape(1, rows))
    loss, query_grad, passage_grad = pl.pallas_call(
        hand_over,
        out_shape=results,
        in_specs=[inside, anywhere, anywhere],
        out_specs=[anywhere] * 3,
        scratch_shapes=[vmem((1, 1), f32), sems((3,))],
        compiler_params=pltpu.CompilerParams(vmem_limit_bytes=1 << 20),
    )(*found)
    return loss.reshape(()), query_grad, passage_grad


def solution(mesh):
    n, m = mesh.shape["dp"], mesh.shape["mp"]
    in_specs = (P("dp", "mp"), P("dp", "mp"), P(None, "dp"), P("dp"))
    out_specs = (P(), P("dp", "mp"), P("dp", "mp"))
    return jax.shard_map(
        functools.partial(per_device, n, m),
        mesh=mesh, in_specs=in_specs, out_specs=out_specs, check_vma=False,
    )
```

```python
import functools
import jax
import jax.numpy as jnp
from jax import lax
from jax.experimental import pallas as pl
from jax.experimental.pallas import tpu as pltpu
from jax.sharding import PartitionSpec as P

PBLK = 16
PB_DEV = 4
MESH = pl.DeviceIdType.MESH
UNROLL = 8
LANES = 128


def flip(index, step, count):
    result, bit = 0, 1
    while bit < count:
        mine, other = (index // bit) % 2, (step // bit) % 2
        result = result + bit * (mine + other - 2 * mine * other)
        bit *= 2
    return result


def wide_slots(count):
    return count // 2 - count // 8


def each(low, high, body):
    if high - low <= UNROLL:
        for step in range(low, high):
            body(step)
    else:
        lax.fori_loop(low, high, lambda step, carry: (body(step), carry)[1], 0)


def kernel(
    n, m, q_hbm, p_hbm, pair_hbm, pos_hbm, loss_ref, qgrad_ref, pgrad_ref, pair_ref, pos_ref, q, p, outgoing, flat, part, shares, turned,
    sent_wide, sent_slim, got_wide, got_slim, loss_dp,
    local_sem, a_send, a_recv, b_send, b_recv, e_send, e_recv, f_send, f_recv,
):
    half = n // 2
    rows = q.shape[0]
    me = lax.axis_index("dp")
    mine = lax.axis_index("mp")

    def remote(src, dst, send, recv, device):
        return pltpu.make_async_remote_copy(
            src_ref=src, dst_ref=dst, send_sem=send, recv_sem=recv,
            device_id=device, device_id_type=MESH,
        )

    def across(step):
        return (flip(me, step, n), mine)

    def beside(step):
        return (me, flip(mine, step, m))

    load_p = pltpu.make_async_copy(p_hbm, p, local_sem.at[0])
    load_q = pltpu.make_async_copy(q_hbm, q, local_sem.at[1])
    load_pair = pltpu.make_async_copy(pair_hbm, pair_ref, local_sem.at[2])
    load_pos = pltpu.make_async_copy(pos_hbm, pos_ref, local_sem.at[3])
    load_pair.start()
    load_p.start()
    load_pos.start()
    load_q.start()
    barrier = pltpu.get_barrier_semaphore()

    def greet(step):
        pl.semaphore_signal(barrier, inc=1, device_id=across(step), device_id_type=MESH)

    each(1, n, greet)
    for step in range(1, m):
        pl.semaphore_signal(barrier, inc=1, device_id=beside(step), device_id_type=MESH)

    def slot(step):
        return pl.ds(step * PBLK, PBLK)

    def chosen(step):
        return p[pair_ref[flip(me, step, n)]]

    load_pair.wait()
    load_p.wait()

    def pack(step):
        outgoing[step] = chosen(step)

    each(1, n, pack)
    flat[0:PBLK, :] = chosen(0)
    pl.semaphore_wait(barrier, n - 1 + m - 1)

    def passage(step):
        return remote(
            outgoing.at[step], flat.at[slot(step)], a_send.at[step], a_recv.at[step], across(step)
        )

    each(1, n, lambda step: passage(step).start())

    load_pos.wait()
    load_q.wait()

    ends = (0, half, half + n // 4, n - n // 8, n)
    chunks = tuple(zip(ends[:-1], ends[1:]))

    def packed(index):
        low, high = chunks[index]
        size = (high - low) * PBLK
        return pl.ds(low * PBLK * 3 // 2, size * 3 // 2), size

    def score(index, step):
        place, _ = packed(index)
        return remote(
            part.at[place], shares.at[step, place], b_send.at[index, step],
            b_recv.at[index, step], beside(step),
        )

    for index, (low, high) in enumerate(chunks):
        each(max(low, 1), high, lambda step: passage(step).wait_recv())
        block = lax.dot_general(
            flat[low * PBLK:high * PBLK, :], q[...], (((1,), (1,)), ((), ())),
            preferred_element_type=jnp.float32,
        )
        place, size = packed(index)
        part[pl.ds(place.start, size), :] = block[:, :LANES]
        part[pl.ds(place.start + size, size // 2), :] = jnp.concatenate(
            [block[:size // 2, LANES:], block[size // 2:, LANES:]], axis=1
        )
        for step in reversed(range(1, m)):
            score(index, step).start()

    def swap(row):
        return jnp.concatenate([row[:, LANES // 2:], row[:, :LANES // 2]], axis=1)

    spots = pos_ref[...] ^ (me * PBLK)
    spots_a = spots[:, :LANES]
    spots_b = jnp.concatenate([spots[:, LANES:], spots[:, LANES:]], axis=1)
    scores_a, scores_b, hits_a, hits_b = [], [], [], []
    for index, (low, high) in enumerate(chunks):
        place, size = packed(index)
        for step in range(1, m):
            score(index, step).wait_recv()
        terms = [part[place, :]] + [shares[step, place, :] for step in range(1, m)]
        while len(terms) > 1:
            terms = [first + second for first, second in zip(terms[::2], terms[1::2])]
        scores_a.append(terms[0][:size])
        scores_b.append(terms[0][size:])
        down = lax.broadcasted_iota(jnp.int32, (size, LANES), 0) + low * PBLK
        hits_a.append(down == spots_a)
        down = lax.broadcasted_iota(jnp.int32, (size // 2, LANES), 0) + low * PBLK
        right = lax.broadcasted_iota(jnp.int32, (size // 2, LANES), 1) // (LANES // 2)
        hits_b.append(down + right * (size // 2) == spots_b)

    def gathered(blocks, combine, reduce):
        return functools.reduce(combine, [reduce(block, axis=0, keepdims=True) for block in blocks])

    def softmax(scores, hits, paired):
        top = gathered(scores, jnp.maximum, jnp.max)
        if paired:
            top = jnp.maximum(top, swap(top))
        raised = [jnp.exp(block - top) for block in scores]
        total = gathered(raised, jnp.add, jnp.sum)
        picked = [jnp.where(hit, block, 0.0) for hit, block in zip(hits, scores)]
        positive = gathered(picked, jnp.add, jnp.sum)
        if paired:
            total = total + swap(total)
            positive = positive + swap(positive)
        inverse = 1.0 / total
        weights = [
            (block * inverse - hit.astype(jnp.float32)).astype(jnp.bfloat16)
            for block, hit in zip(raised, hits)
        ]
        return weights, top + jnp.log(total) - positive

    weights_a, losses_a = softmax(scores_a, hits_a, False)
    weights_b, losses_b = softmax(scores_b, hits_b, True)
    for (low, high), first, second in zip(chunks, weights_a, weights_b):
        start, size = low * PBLK, (high - low) * PBLK
        turned[pl.ds(start, size), pl.ds(0, LANES)] = first
        rest = pl.ds(LANES, LANES // 2)
        turned[pl.ds(start, size // 2), rest] = second[:, :LANES // 2]
        turned[pl.ds(start + size // 2, size // 2), rest] = second[:, LANES // 2:]

    wide = wide_slots(n)

    def gradient(step, slim):
        if slim:
            source, target = sent_slim.at[step - wide], got_slim.at[step - wide]
        else:
            source, target = sent_wide.at[step], got_wide.at[step]
        return remote(source, target, e_send.at[step], e_recv.at[step], across(step))

    group = min(half, 4)

    def give(index, slim):
        block = turned[pl.ds(index * group * PBLK, group * PBLK), :]
        result = jnp.dot(block, q[...], preferred_element_type=jnp.float32)
        result = result.reshape(group, PBLK, q.shape[1])
        for place in range(group):
            step = index * group + place
            fixed = isinstance(step, int)
            narrow = step >= wide if fixed else slim
            if narrow:
                sent_slim[step - wide] = result[place].astype(jnp.bfloat16)
            else:
                sent_wide[step] = result[place]
            if not fixed:
                pl.when(step > 0)(lambda step=step: gradient(step, narrow).start())
            elif step:
                gradient(step, narrow).start()

    wide_groups = -(-wide // group)
    each(half // group, n // group, lambda index: give(index, True))
    each(wide_groups, half // group, lambda index: give(index, True))
    each(0, wide_groups, lambda index: give(index, False))

    losses = losses_a + 0.5 * losses_b
    loss_dp[0] = jnp.broadcast_to(jnp.sum(losses, axis=1, keepdims=True), loss_dp.shape[1:])

    def loss_across(step):
        return remote(
            loss_dp.at[0], loss_dp.at[step], f_send.at[step], f_recv.at[step], across(step)
        )

    each(1, n, lambda step: loss_across(step).start())

    qgrad_ref[...] = lax.dot_general(
        turned[...], flat[...], (((0,), (0,)), ((), ())), preferred_element_type=jnp.float32
    )

    each(1, n, lambda step: passage(step).wait_send())
    for index in range(len(chunks)):
        for step in range(1, m):
            score(index, step).wait_send()
    pgrad_ref[...] = jnp.zeros_like(pgrad_ref)

    def collect(step, block):
        pick = jnp.full(block.shape, pair_ref[flip(me, step, n)], jnp.int32)
        for place in range(PB_DEV):
            pgrad_ref[pl.ds(place * PBLK, PBLK), :] += jnp.where(pick == place, block, 0.0)

    def take_wide(step):
        gradient(step, False).wait_recv()
        collect(step, got_wide[step])

    def take_slim(step):
        gradient(step, True).wait_recv()
        collect(step, got_slim[step - wide].astype(jnp.float32))

    collect(0, sent_wide[0])
    each(1, wide, take_wide)
    each(wide, n, take_slim)
    each(1, n, lambda step: loss_across(step).wait_recv())
    losses = loss_dp[...]
    while losses.shape[0] > 1:
        losses = losses.reshape(losses.shape[0] // 2, 2, *losses.shape[1:])
        losses = losses[:, 0] + losses[:, 1]
    loss_ref[...] = losses[0] / (rows * n)

    each(1, n, lambda step: loss_across(step).wait_send())
    each(1, wide, lambda step: gradient(step, False).wait_send())
    each(wide, n, lambda step: gradient(step, True).wait_send())


def hand_over(loss_in, qgrad_in, pgrad_in, loss_out, qgrad_out, pgrad_out, loss, sems):
    loss[...] = loss_in[0:1, 0:1]
    pairs = ((qgrad_in, qgrad_out), (pgrad_in, pgrad_out), (loss, loss_out))
    copies = [
        pltpu.make_async_copy(source, target, sems.at[index])
        for index, (source, target) in enumerate(pairs)
    ]
    for copy in copies:
        copy.start()
    for copy in copies:
        copy.wait()


def per_device(n, m, queries, passages, pair_block, positives):
    rows, width = queries.shape
    wide, cands = wide_slots(n), n * PBLK
    vmem, sems = pltpu.VMEM, pltpu.SemaphoreType.DMA
    bf16, f32 = jnp.bfloat16, jnp.float32
    results = [
        jax.ShapeDtypeStruct((1, 1), f32),
        jax.ShapeDtypeStruct((rows, width), f32),
        jax.ShapeDtypeStruct(passages.shape, f32),
    ]
    held = [vmem((8, 128), f32), vmem((rows, width), f32), vmem(passages.shape, f32)]
    scratch = [
        pltpu.SMEM((n,), jnp.int32),
        vmem((1, rows), jnp.int32),
        vmem((rows, width), bf16),
        vmem((PB_DEV, PBLK, width), bf16),
        vmem((n, PBLK, width), bf16),
        vmem((cands, width), bf16),
        vmem((cands * 3 // 2, LANES), f32),
        vmem((m, cands * 3 // 2, LANES), f32),
        vmem((cands, rows), bf16),
        vmem((wide, PBLK, width), f32),
        vmem((n - wide, PBLK, width), bf16),
        vmem((wide, PBLK, width), f32),
        vmem((n - wide, PBLK, width), bf16),
        vmem((n, 8, 128), f32),
        sems((4,)),
        sems((n,)), sems((n,)), sems((4, m)), sems((4, m)),
        sems((n,)), sems((n,)), sems((n,)), sems((n,)),
    ]
    anywhere = pl.BlockSpec(memory_space=pl.ANY)
    inside = pl.BlockSpec(memory_space=pltpu.VMEM)
    found = pl.pallas_call(
        functools.partial(kernel, n, m),
        out_shape=held,
        in_specs=[anywhere] * 4,
        out_specs=[inside] * 3,
        scratch_shapes=scratch,
        compiler_params=pltpu.CompilerParams(
            collective_id=0, has_side_effects=True,
            vmem_limit_bytes=60 << 20,
        ),
    )(queries, passages.reshape(PB_DEV, PBLK, width), pair_block.reshape(n),
      positives.reshape(1, rows))
    loss, query_grad, passage_grad = pl.pallas_call(
        hand_over,
        out_shape=results,
        in_specs=[inside, anywhere, anywhere],
        out_specs=[anywhere] * 3,
        scratch_shapes=[vmem((1, 1), f32), sems((3,))],
        compiler_params=pltpu.CompilerParams(vmem_limit_bytes=1 << 20),
    )(*found)
    return loss.reshape(()), query_grad, passage_grad


def solution(mesh):
    n, m = mesh.shape["dp"], mesh.shape["mp"]
    in_specs = (P("dp", "mp"), P("dp", "mp"), P(None, "dp"), P("dp"))
    out_specs = (P(), P("dp", "mp"), P("dp", "mp"))
    return jax.shard_map(
        functools.partial(per_device, n, m),
        mesh=mesh, in_specs=in_specs, out_specs=out_specs, check_vma=False,
    )
```
